512 devices in a mesh: grp: 8 (over y_lo, core), night: 64 (over x, y_hi, z).
Axes of the slice: x: 4, y: 8 (y_hi: 2, y_lo: 4; y = y_hi * 4 + y_lo), z: 8, core: 2. Of those that a mesh axis runs over, the one named last changes fastest.
Arguments:
- sensor_reading_array: float32 [512, 16, 65536], P('night', None, 'grp'), may hold values from -16 to 16
- starting_evening_loadings: float32 [64, 512], P(None, 'night'), may hold values from -6 to 6
- starting_span_loadings: float32 [64, 16], replicated, may hold values from -6 to 6
Outputs:
- updated_sensor_loadings: float32 [64, 65536], P(None, ('grp', 'night'))
- updated_evening_loadings: float32 [64, 512], P(None, 'night')
- updated_span_loadings: float32 [64, 16], replicated
The draws below stay inside these ranges and needn't reach their ends.
All inputs are finite; a program needn't handle non-finite values.
Results may differ from the reference program's by a relative error of at most 0.000075.
Values sent between devices are 32-bit elements; how exact they have to be, the bound alone decides.
No kernel may reach another device: no remote copies, remote signals or barrier semaphores. Data moves between devices by JAX's collectives and lax.ppermute only.
A program may use at most 64 MiB of HBM per device.

```python
import jax
import jax.numpy as jnp
from jax import lax

COMPONENT_TOTAL = 64
SPANS_PER_EVENING = 16
SENSOR_TOTAL = 65536
EVENING_TOTAL = 512


def strengthened(array, key, source, target, parts, factor):
    def block_of(axis_at):
        return (jnp.arange(array.shape[axis_at]) // (array.shape[axis_at] // parts)).reshape((-1,) + (1,) * (array.ndim - 1 - axis_at))

    first = jax.random.permutation(key, parts)[block_of(target)]
    second = (block_of(target) + parts // 2) % parts
    return jnp.where((block_of(source) == first) | (block_of(source) == second), factor * array, array)


def levels(own_key, shape, cuts, least, largest):
    def one(dim, parts):
        heights = jax.random.uniform(jax.random.fold_in(jax.random.fold_in(own_key, 6), dim), (parts,), jnp.float32, least / len(cuts), largest / len(cuts))
        return jnp.repeat(jnp.exp(heights), shape[dim] // parts).reshape((-1,) + (1,) * (len(shape) - dim - 1))

    factor_of = one(*cuts[0])
    for cut in cuts[1:]:
        factor_of = factor_of * one(*cut)
    return factor_of


def noise(own_key, extent, width, bound, pieces=(), kind=jnp.bfloat16):
    values = jax.random.normal(own_key, extent, jnp.float32) * width
    if len(pieces) > 0:
        values = levels(own_key, extent, pieces, -0.22, 0.18) * values
    return jnp.clip(values, min=-bound, max=bound).astype(kind)


def bell_draw_with(own_key, extent, scale, reach, pieces, heavy, dtype=jnp.bfloat16):
    array = scale * jax.random.normal(own_key, extent, jnp.float32)
    if pieces:
        array = array * levels(own_key, extent, pieces, -0.22, 0.18)
    return jnp.clip(strengthened(array, jax.random.fold_in(own_key, 3), *heavy), -reach, reach).astype(dtype)


def setup_inputs(seed: int = 0) -> dict:
    key_of = jax.random.split(jax.random.key(seed), 4)
    sensor_reading_array = bell_draw_with(key_of[0], (EVENING_TOTAL, SPANS_PER_EVENING, SENSOR_TOTAL), 1.0, 16.0, ((0, 64), (2, 8)), (0, 2, 64, 4.0), jnp.float32)
    starting_evening_loadings = noise(key_of[1], (COMPONENT_TOTAL, EVENING_TOTAL), 1.0, 6.0, ((1, 64),), jnp.float32)
    starting_span_loadings = noise(key_of[2], (COMPONENT_TOTAL, SPANS_PER_EVENING), 1.0, 6.0, (), jnp.float32)
    return {"sensor_reading_array": sensor_reading_array, "starting_evening_loadings": starting_evening_loadings, "starting_span_loadings": starting_span_loadings}


FULL_ACCURACY = lax.Precision.HIGHEST
EPSILON_SHIFT = 1e-06

def normal_equation_answer(gram_matrix, right_side):
    factor = jnp.linalg.cholesky(gram_matrix)
    return jax.scipy.linalg.cho_solve((factor, True), right_side)

def normalised_loadings(raw_cols):
    component_norms = jnp.sqrt(lax.optimization_barrier(jnp.mean(raw_cols * raw_cols, axis=1)) + EPSILON_SHIFT)
    return raw_cols / component_norms[:, None]

def reference(sensor_reading_array, starting_evening_loadings, starting_span_loadings):
    unfolded_readings = sensor_reading_array.reshape(EVENING_TOTAL * SPANS_PER_EVENING, SENSOR_TOTAL)
    span_inner_matrix = jnp.dot(starting_span_loadings, starting_span_loadings.T, precision=FULL_ACCURACY)
    evening_cross_matrix = jnp.dot(starting_evening_loadings, starting_evening_loadings.T, precision=FULL_ACCURACY)
    columnwise_kron = (starting_evening_loadings[:, :, None] * starting_span_loadings[:, None, :]).reshape(COMPONENT_TOTAL, EVENING_TOTAL * SPANS_PER_EVENING)
    sensor_kron_matrix = jnp.dot(columnwise_kron, unfolded_readings, precision=FULL_ACCURACY)
    updated_sensor_loadings = normalised_loadings(normal_equation_answer(evening_cross_matrix * span_inner_matrix, sensor_kron_matrix))
    sensor_inner_matrix = jnp.dot(updated_sensor_loadings, updated_sensor_loadings.T, precision=FULL_ACCURACY)
    mode_reduced_matrix = jnp.dot(unfolded_readings, updated_sensor_loadings.T, precision=FULL_ACCURACY).reshape(EVENING_TOTAL, SPANS_PER_EVENING, COMPONENT_TOTAL)
    evening_mode_matrix = jnp.einsum('jkr,rk->rj', mode_reduced_matrix, starting_span_loadings, precision=FULL_ACCURACY)
    updated_evening_loadings = normalised_loadings(normal_equation_answer(sensor_inner_matrix * span_inner_matrix, evening_mode_matrix))
    evening_inner_matrix = jnp.dot(updated_evening_loadings, updated_evening_loadings.T, precision=FULL_ACCURACY)
    span_mode_matrix = jnp.einsum('jkr,rj->rk', mode_reduced_matrix, updated_evening_loadings, precision=FULL_ACCURACY)
    updated_span_loadings = normalised_loadings(normal_equation_answer(sensor_inner_matrix * evening_inner_matrix, span_mode_matrix))
    return (updated_sensor_loadings, updated_evening_loadings, updated_span_loadings)
```

```python
import jax
import jax.numpy as jnp
import numpy as np
from jax import lax
from jax.sharding import Mesh, PartitionSpec as P

FULL = lax.Precision.HIGHEST
EPS = 1e-06
GRP = ("ylo", "core")
NIGHT = ("x", "yhi", "z")
SPLIT = {"ylo": 4, "core": 2, "x": 4, "yhi": 2, "z": 8}


def spd_inverse(gram):
    factor = jnp.linalg.cholesky(gram)
    low = jax.scipy.linalg.solve_triangular(
        factor, jnp.eye(gram.shape[0], dtype=gram.dtype), lower=True
    )
    return jnp.dot(low.T, low, precision=FULL)


def exchange(blocks, axis):
    return lax.all_to_all(blocks, axis, 0, 0, tiled=True)


def exchange_sum(blocks, axis):
    return jnp.sum(exchange(blocks, axis), axis=0)


def spread(block, axis):
    size = lax.axis_size(axis)
    return exchange(jnp.broadcast_to(block, (size,) + block.shape), axis)


def on_device(readings, evenings, spans):
    rank, own_nights = evenings.shape
    nights, intervals, meters = readings.shape
    nx, nyhi, nz = (lax.axis_size(a) for a in NIGHT)
    night_devices = nx * nyhi * nz
    share = meters // night_devices
    meter_total = meters * lax.axis_size(GRP)
    night_total = nights * night_devices
    x2 = readings.reshape(nights * intervals, meters)

    gram_c = jnp.dot(spans, spans.T, precision=FULL)
    all_evenings = spread(evenings, NIGHT)
    gram_b = jnp.einsum("nrj,nsj->rs", all_evenings, all_evenings, precision=FULL)
    inverse_a = spd_inverse(gram_b * gram_c)

    kron = (evenings[:, :, None] * spans[:, None, :]).reshape(rank, nights * intervals)
    partial = jnp.dot(kron, x2, precision=FULL)
    blocks = partial.reshape(rank, nx, nyhi, nz, share).transpose(1, 3, 2, 0, 4)
    blocks = exchange_sum(blocks, "x")
    blocks = exchange_sum(blocks, "z")
    own = exchange_sum(blocks, "yhi")

    own_raw = jnp.dot(inverse_a, own, precision=FULL)
    full = spread(spread(spread(own_raw, "yhi"), "z"), "x")
    full = full.transpose(3, 0, 2, 1, 4).reshape(rank, meters)

    contracted = jnp.dot(x2, full.T, precision=FULL)
    gram_raw = jnp.dot(full, full.T, precision=FULL)
    summed = jnp.sum(spread(jnp.concatenate([contracted, gram_raw], axis=0), GRP), axis=0)
    gram_raw = summed[nights * intervals :]
    scale_a = jnp.sqrt(jnp.diagonal(gram_raw) / meter_total + EPS)
    own_cols = own_raw / scale_a[:, None]
    gram_a = gram_raw / scale_a[:, None] / scale_a[None, :]
    contracted = (summed[: nights * intervals] / scale_a[None, :]).reshape(
        nights, intervals, rank
    )

    night_products = jnp.einsum("jkr,rk->rj", contracted, spans, precision=FULL)
    night_raw = jnp.dot(spd_inverse(gram_a * gram_c), night_products, precision=FULL)
    interval_part = jnp.einsum("jkr,rj->rk", contracted, night_raw, precision=FULL)
    gathered = spread(jnp.concatenate([night_raw, interval_part], axis=1), NIGHT)
    all_nights = gathered[:, :, :nights]
    gram_raw = jnp.einsum("nrj,nsj->rs", all_nights, all_nights, precision=FULL)
    scale_b = jnp.sqrt(jnp.diagonal(gram_raw) / night_total + EPS)
    evenings_out = night_raw / scale_b[:, None]
    gram_n = gram_raw / scale_b[:, None] / scale_b[None, :]
    interval_products = jnp.sum(gathered[:, :, nights:], axis=0) / scale_b[:, None]
    spans_raw = jnp.dot(spd_inverse(gram_a * gram_n), interval_products, precision=FULL)
    scale_c = jnp.sqrt(jnp.mean(spans_raw * spans_raw, axis=1) + EPS)
    return own_cols, evenings_out, spans_raw / scale_c[:, None]


def solution(mesh):
    fine = Mesh(
        np.asarray(mesh.devices).reshape(tuple(SPLIT.values())), tuple(SPLIT)
    )
    in_specs = (P(NIGHT, None, GRP), P(None, NIGHT), P())
    out_specs = (P(None, GRP + NIGHT), P(None, NIGHT), P())
    return jax.shard_map(
        on_device, mesh=fine, in_specs=in_specs, out_specs=out_specs, check_vma=False
    )
```

```python
import functools

import jax
import jax.numpy as jnp
import numpy as np
from jax import lax
from jax.experimental import pallas as pl
from jax.experimental.pallas import tpu as pltpu
from jax.sharding import Mesh, PartitionSpec as P

FULL = lax.Precision.HIGHEST
EPS = 1e-06
GRP = ("ylo", "core")
NIGHT = ("x", "yhi", "z")
ZY = ("z", "yhi")
SPLIT = {"ylo": 4, "core": 2, "x": 4, "yhi": 2, "z": 8}
VMEM = pl.BlockSpec(memory_space=pltpu.VMEM)
PARAMS = pltpu.CompilerParams(vmem_limit_bytes=40 * 1024 * 1024)


def f32(*shape):
    return jax.ShapeDtypeStruct(shape, jnp.float32)


def call(body, outs, *operands):
    return pl.pallas_call(
        body,
        out_shape=outs,
        in_specs=[VMEM] * len(operands),
        out_specs=jax.tree.map(lambda _: VMEM, outs),
        compiler_params=PARAMS,
    )(*operands)


def block_order(nx, nyhi, nz):
    return [
        ((x * nyhi + y) * nz + z, (x * nz + z) * nyhi + y)
        for x in range(nx)
        for y in range(nyhi)
        for z in range(nz)
    ]


def partial_body(order, nz, kron_ref, x_ref, out_ref):
    share = out_ref.shape[-1]
    for first in range(0, len(order), nz):
        columns = pl.ds(first * share, nz * share)
        product = jnp.dot(
            kron_ref[...], x_ref[:, columns], precision=FULL,
            preferred_element_type=jnp.float32,
        )
        for i in range(nz):
            out_ref[order[first + i][1]] = product[:, i * share : (i + 1) * share]


def contract_body(order, nz, copies, x_ref, a_ref, out_ref):
    rank, share = a_ref.shape[1:]
    rows = x_ref.shape[0]
    total = jnp.zeros((rows + rank, rank), jnp.float32)
    for first in range(0, len(order), nz):
        loadings = jnp.concatenate(
            [a_ref[order[first + i][1]] for i in range(nz)], axis=1
        )
        left = jnp.concatenate(
            [x_ref[:, pl.ds(first * share, nz * share)], loadings], axis=0
        )
        total += lax.dot_general(
            left, loadings, (((1,), (1,)), ((), ())), precision=FULL,
            preferred_element_type=jnp.float32,
        )
    half, quarter = rows // 2, rank // 2
    packed = jnp.concatenate(
        [
            jnp.concatenate([total[:half], total[half:rows]], axis=1),
            jnp.concatenate([total[rows : rows + quarter], total[rows + quarter :]], axis=1),
        ],
        axis=0,
    )
    for i in range(copies):
        out_ref[i] = packed


def right_divide(gram, right):
    size = gram.shape[0]
    work = jnp.concatenate([gram, right], axis=0)
    lane = lax.broadcasted_iota(jnp.int32, (1, size), 1)
    for p in range(size):
        at = p % 8
        row = work[at : at + 1, :]
        here = lane == p
        factor = jnp.where(here, -1.0, row) / row[:, p : p + 1]
        work = jnp.where(here, 0.0, work) - work[:, p : p + 1] * factor
        if at == 7:
            work = work[8:]
    return work


def diagonals(gram):
    size = gram.shape[0]
    mask = lax.broadcasted_iota(jnp.int32, (size, size), 0) == lax.broadcasted_iota(
        jnp.int32, (size, size), 1
    )
    kept = jnp.where(mask, gram, 0.0)
    return jnp.sum(kept, axis=0, keepdims=True), jnp.sum(kept, axis=1, keepdims=True)


def night_body(meters, got_ref, gram_c_ref, spans_t_ref, send_ref, raw_ref, gram_ref, scale_ref):
    rank = gram_c_ref.shape[0]
    intervals = spans_t_ref.shape[0]
    got = got_ref[0]
    for i in range(1, got_ref.shape[0]):
        got += got_ref[i]
    half = got.shape[0] - rank // 2
    contracted = jnp.concatenate([got[:half, :rank], got[:half, rank:]], axis=0)
    gram = jnp.concatenate([got[half:, :rank], got[half:, rank:]], axis=0)
    along, down = diagonals(gram)
    along = jnp.sqrt(along / meters + EPS)
    down = jnp.sqrt(down / meters + EPS)
    gram = gram / down / along
    contracted = (contracted / along).reshape(-1, intervals, rank)
    products = jnp.sum(contracted * spans_t_ref[...][None], axis=1)
    raw = right_divide(gram * gram_c_ref[...], products)
    interval = contracted[0] * raw[0:1]
    for j in range(1, raw.shape[0]):
        interval += contracted[j] * raw[j : j + 1]
    packed = jnp.concatenate(
        [
            jnp.concatenate([raw, raw], axis=1),
            jnp.concatenate([interval[: intervals // 2], interval[intervals // 2 :]], axis=1),
        ],
        axis=0,
    )
    for i in range(send_ref.shape[0]):
        send_ref[i] = packed
    raw_ref[...] = raw
    gram_ref[...] = gram
    scale_ref[...] = down


def transposed(block):
    rows, columns = block.shape
    block = jnp.concatenate([block, jnp.zeros((128 - rows, columns), jnp.float32)], axis=0)
    block = jnp.concatenate([block, jnp.zeros((128, 128 - columns), jnp.float32)], axis=1)
    return block.T[:columns, :rows]


def span_body(night_total, got_ref, raw_ref, gram_ref, evenings_ref, spans_ref):
    rank = gram_ref.shape[0]
    nights = raw_ref.shape[0]
    everything = got_ref[:, :nights, :][:, :, :rank].reshape(-1, rank)
    gram = lax.dot_general(
        everything, everything, (((0,), (0,)), ((), ())), precision=FULL,
        preferred_element_type=jnp.float32,
    )
    interval = jnp.sum(got_ref[:, nights:, :], axis=0)
    along, down = diagonals(gram)
    along = jnp.sqrt(along / night_total + EPS)
    down = jnp.sqrt(down / night_total + EPS)
    gram = gram / down / along
    interval = jnp.concatenate([interval[:, :rank], interval[:, rank:]], axis=0) / along
    raw = right_divide(gram * gram_ref[...], interval)
    scale = jnp.sqrt(jnp.mean(raw * raw, axis=0, keepdims=True) + EPS)
    evenings_ref[...] = transposed(raw_ref[...] / along)
    spans_ref[...] = transposed(raw / scale)


def spd_inverse(gram):
    factor = jnp.linalg.cholesky(gram)
    low = jax.scipy.linalg.solve_triangular(
        factor, jnp.eye(gram.shape[0], dtype=gram.dtype), lower=True
    )
    return jnp.dot(low.T, low, precision=FULL)


def exchange(blocks, axis):
    return lax.all_to_all(blocks, axis, 0, 0, tiled=True)


def exchange_sum(blocks, axis):
    size = lax.axis_size(axis)
    got = exchange(blocks, axis)
    return jnp.sum(got.reshape((size, -1) + got.shape[1:]), axis=0)


def spread(block, axis):
    size = lax.axis_size(axis)
    return exchange(jnp.broadcast_to(block, (size,) + block.shape), axis)


def on_device(readings, evenings, spans):
    rank, nights = evenings.shape
    _, intervals, meters = readings.shape
    nx, nyhi, nz = (lax.axis_size(a) for a in NIGHT)
    night_devices = nx * nyhi * nz
    share = meters // night_devices
    copies = lax.axis_size(GRP)
    order = block_order(nx, nyhi, nz)
    x2 = readings.reshape(nights * intervals, meters)

    gram_c = jnp.dot(spans, spans.T, precision=FULL)
    all_evenings = spread(evenings, NIGHT)
    gram_b = jnp.einsum("nrj,nsj->rs", all_evenings, all_evenings, precision=FULL)
    inverse_a = spd_inverse(gram_b * gram_c)

    kron = (evenings[:, :, None] * spans[:, None, :]).reshape(rank, nights * intervals)
    blocks = call(
        functools.partial(partial_body, order, nz), f32(night_devices, rank, share), kron, x2
    )
    blocks = exchange_sum(blocks, "x")
    own = exchange_sum(blocks, ZY)[0]
    own_raw = jnp.dot(inverse_a, own, precision=FULL)
    full = spread(spread(own_raw, ZY), "x").reshape(night_devices, rank, share)

    packed = call(
        functools.partial(contract_body, order, nz, copies),
        f32(copies, (nights * intervals + rank) // 2, 2 * rank), x2, full,
    )
    send, raw, gram_a, scale = call(
        functools.partial(night_body, meters * copies),
        (
            f32(night_devices, nights + intervals // 2, 2 * rank),
            f32(nights, rank), f32(rank, rank), f32(rank, 1),
        ),
        exchange(packed, GRP), gram_c, spans.T,
    )
    evenings_out, spans_out = call(
        functools.partial(span_body, nights * night_devices),
        (f32(rank, nights), f32(rank, intervals)),
        exchange(send, NIGHT), raw, gram_a,
    )
    return own_raw / scale, evenings_out, spans_out


def solution(mesh):
    fine = Mesh(
        np.asarray(mesh.devices).reshape(tuple(SPLIT.values())), tuple(SPLIT)
    )
    in_specs = (P(NIGHT, None, GRP), P(None, NIGHT), P())
    out_specs = (P(None, GRP + NIGHT), P(None, NIGHT), P())
    return jax.shard_map(
        on_device, mesh=fine, in_specs=in_specs, out_specs=out_specs, check_vma=False
    )
```

```python
import functools

import jax
import jax.numpy as jnp
import numpy as np
from jax import lax
from jax.experimental import pallas as pl
from jax.experimental.pallas import tpu as pltpu
from jax.sharding import Mesh, PartitionSpec as P

FULL = lax.Precision.HIGHEST
EPS = 1e-06
GRP = ("ylo", "core")
NIGHT = ("x", "yhi", "z")
ZY = ("z", "yhi")
SPLIT = {"ylo": 4, "core": 2, "x": 4, "yhi": 2, "z": 8}
VMEM = pl.BlockSpec(memory_space=pltpu.VMEM)
STREAM = pltpu.CompilerParams(vmem_limit_bytes=60 * 1024 * 1024)
PARAMS = pltpu.CompilerParams(vmem_limit_bytes=40 * 1024 * 1024)


def f32(*shape):
    return jax.ShapeDtypeStruct(shape, jnp.float32)


def call(body, outs, *operands):
    return pl.pallas_call(
        body,
        out_shape=outs,
        in_specs=[VMEM] * len(operands),
        out_specs=jax.tree.map(lambda _: VMEM, outs),
        compiler_params=PARAMS,
    )(*operands)


def partial_body(nyhi, nz, kron_ref, x_ref, out_ref):
    rank, share = kron_ref.shape[0], x_ref.shape[1] // (nyhi * nz)
    for y in range(nyhi):
        product = jnp.dot(
            kron_ref[...], x_ref[:, y * nz * share : (y + 1) * nz * share], precision=FULL,
            preferred_element_type=jnp.float32,
        )
        for z in range(nz):
            out_ref[0, z * nyhi + y] = product[:, z * share : (z + 1) * share]


def inverse_body(gram_b_ref, gram_c_ref, out_ref):
    gram = gram_b_ref[...] * gram_c_ref[...]
    out_ref[...] = right_divide(gram, identity(gram.shape[0]))


def join_body(got_ref, gram_ref, out_ref, gram_out_ref):
    for n in range(out_ref.shape[0]):
        block = got_ref[0, n]
        for i in range(1, got_ref.shape[0]):
            block += got_ref[i, n]
        out_ref[n] = block
    gram_out_ref[...] = gram_ref[...]


def own_body(got_ref, gram_ref, own_ref, send_ref, gram_out_ref):
    products = got_ref[0]
    for i in range(1, got_ref.shape[0]):
        products += got_ref[i]
    own_ref[...] = products
    for i in range(send_ref.shape[0]):
        send_ref[i] = products
    gram_out_ref[...] = gram_ref[...]


def apply_body(inverse_ref, own_ref, got_ref, own_out_ref, send_ref):
    dot = functools.partial(jnp.dot, precision=FULL, preferred_element_type=jnp.float32)
    inverse = inverse_ref[...]
    own_out_ref[...] = dot(inverse, own_ref[...])
    step = min(8, got_ref.shape[0])
    width = got_ref.shape[-1]
    for first in range(0, got_ref.shape[0], step):
        products = jnp.concatenate([got_ref[first + i] for i in range(step)], axis=1)
        loadings = dot(inverse, products)
        for i in range(step):
            block = loadings[:, i * width : (i + 1) * width]
            for k in range(send_ref.shape[0]):
                send_ref[k, first + i] = block


def identity(size):
    return (
        lax.broadcasted_iota(jnp.int32, (size, size), 0)
        == lax.broadcasted_iota(jnp.int32, (size, size), 1)
    ).astype(jnp.float32)


def contract_body(nyhi, nz, x_ref, a_ref, out_ref, total_ref):
    rank, share = a_ref.shape[1:]
    rows = x_ref.shape[0]
    step = pl.program_id(0)

    @pl.when(step == 0)
    def _():
        total_ref[...] = jnp.zeros_like(total_ref)

    total = total_ref[...]
    for y in range(nyhi):
        loadings = jnp.concatenate([a_ref[z * nyhi + y] for z in range(nz)], axis=1)
        left = jnp.concatenate(
            [x_ref[:, y * nz * share : (y + 1) * nz * share], loadings], axis=0
        )
        total += lax.dot_general(
            left, loadings, (((1,), (1,)), ((), ())), precision=FULL,
            preferred_element_type=jnp.float32,
        )
    total_ref[...] = total

    @pl.when(step == pl.num_programs(0) - 1)
    def _():
        half, quarter = rows // 2, rank // 2
        packed = jnp.concatenate(
            [
                jnp.concatenate([total[:half], total[half:rows]], axis=1),
                jnp.concatenate(
                    [total[rows : rows + quarter], total[rows + quarter :]], axis=1
                ),
            ],
            axis=0,
        )
        for i in range(out_ref.shape[0]):
            out_ref[i] = packed


def right_divide(gram, right):
    size = gram.shape[0]
    work = jnp.concatenate([gram, right], axis=0)
    lane = lax.broadcasted_iota(jnp.int32, (1, size), 1)
    for p in range(size):
        at = p % 8
        row = work[at : at + 1, :]
        here = lane == p
        factor = jnp.where(here, -1.0, row) / row[:, p : p + 1]
        work = jnp.where(here, 0.0, work) - work[:, p : p + 1] * factor
        if at == 7:
            work = work[8:]
    return work


def diagonals(gram):
    size = gram.shape[0]
    mask = lax.broadcasted_iota(jnp.int32, (size, size), 0) == lax.broadcasted_iota(
        jnp.int32, (size, size), 1
    )
    kept = jnp.where(mask, gram, 0.0)
    return jnp.sum(kept, axis=0, keepdims=True), jnp.sum(kept, axis=1, keepdims=True)


def night_body(meters, got_ref, gram_c_ref, spans_t_ref, send_ref, raw_ref, gram_ref, scale_ref):
    rank = gram_c_ref.shape[0]
    intervals = spans_t_ref.shape[0]
    got = got_ref[0]
    for i in range(1, got_ref.shape[0]):
        got += got_ref[i]
    half = got.shape[0] - rank // 2
    contracted = jnp.concatenate([got[:half, :rank], got[:half, rank:]], axis=0)
    gram = jnp.concatenate([got[half:, :rank], got[half:, rank:]], axis=0)
    along, down = diagonals(gram)
    along = jnp.sqrt(along / meters + EPS)
    down = jnp.sqrt(down / meters + EPS)
    gram = gram / down / along
    contracted = (contracted / along).reshape(-1, intervals, rank)
    products = jnp.sum(contracted * spans_t_ref[...][None], axis=1)
    raw = right_divide(gram * gram_c_ref[...], products)
    interval = contracted[0] * raw[0:1]
    for j in range(1, raw.shape[0]):
        interval += contracted[j] * raw[j : j + 1]
    packed = jnp.concatenate(
        [
            jnp.concatenate([raw, raw], axis=1),
            jnp.concatenate([interval[: intervals // 2], interval[intervals // 2 :]], axis=1),
        ],
        axis=0,
    )
    for i in range(send_ref.shape[0]):
        send_ref[i] = packed
    raw_ref[...] = raw
    gram_ref[...] = gram
    scale_ref[...] = down


def span_body(night_total, got_ref, raw_ref, gram_ref, evenings_ref, spans_ref):
    rank = gram_ref.shape[0]
    nights = raw_ref.shape[0]
    everything = got_ref[:, :nights, :][:, :, :rank].reshape(-1, rank)
    gram = lax.dot_general(
        everything, everything, (((0,), (0,)), ((), ())), precision=FULL,
        preferred_element_type=jnp.float32,
    )
    interval = jnp.sum(got_ref[:, nights:, :], axis=0)
    along, down = diagonals(gram)
    along = jnp.sqrt(along / night_total + EPS)
    down = jnp.sqrt(down / night_total + EPS)
    gram = gram / down / along
    interval = jnp.concatenate([interval[:, :rank], interval[:, rank:]], axis=0) / along
    raw = right_divide(gram * gram_ref[...], interval)
    scale = jnp.sqrt(jnp.mean(raw * raw, axis=0, keepdims=True) + EPS)
    evenings_ref[...] = raw_ref[...] / along
    spans_ref[...] = raw / scale


def exchange(blocks, axis):
    return lax.all_to_all(blocks, axis, 0, 0, tiled=True)


def paired(total, axis, step):
    size = lax.axis_size(axis)
    return total + lax.ppermute(total, axis, [(i, i ^ step) for i in range(size)])


def butterfly(total, axis, step=1):
    while step < lax.axis_size(axis):
        total = paired(total, axis, step)
        step *= 2
    return total


def on_device(readings, evenings, spans):
    rank, nights = evenings.shape
    _, intervals, meters = readings.shape
    nx, nyhi, nz = (lax.axis_size(a) for a in NIGHT)
    night_devices = nx * nyhi * nz
    share = meters // night_devices
    copies = lax.axis_size(GRP)
    x2 = readings.reshape(nights * intervals, meters)
    gram_c = jnp.dot(spans, spans.T, precision=FULL)
    kron = (evenings[:, :, None] * spans[:, None, :]).reshape(rank, nights * intervals)
    places = nyhi * nz
    blocks = pl.pallas_call(
        functools.partial(partial_body, nyhi, nz),
        out_shape=f32(nx, places, rank, share),
        grid=(nx,),
        in_specs=[
            pl.BlockSpec((rank, nights * intervals), lambda i: (0, 0)),
            pl.BlockSpec((nights * intervals, places * share), lambda i: (0, i)),
        ],
        out_specs=pl.BlockSpec((1, places, rank, share), lambda i: (i, 0, 0, 0)),
        compiler_params=STREAM,
    )(kron, x2)

    square = f32(rank, rank)
    gram_b = jnp.dot(evenings, evenings.T, precision=FULL)
    gram_b = butterfly(gram_b, "z")
    joined, gram_b = call(
        join_body, (f32(places, rank, share), square), exchange(blocks, "x"), gram_b
    )
    gram_b = butterfly(gram_b, "yhi")
    gram_b = paired(gram_b, "x", 1)
    own, send, gram_b = call(
        own_body, (f32(rank, share), f32(places, rank, share), square),
        exchange(joined, ZY), gram_b,
    )
    gram_b = butterfly(gram_b, "x", 2)
    inverse = call(inverse_body, square, gram_b, gram_c)
    own_raw, send = call(
        apply_body, (f32(rank, share), f32(nx, places, rank, share)),
        inverse, own, exchange(send, ZY),
    )
    full = exchange(send, "x").reshape(night_devices, rank, share)

    packed_shape = (copies, (nights * intervals + rank) // 2, 2 * rank)
    packed = pl.pallas_call(
        functools.partial(contract_body, nyhi, nz),
        out_shape=f32(*packed_shape),
        grid=(nx,),
        in_specs=[
            pl.BlockSpec((nights * intervals, places * share), lambda i: (0, i)),
            pl.BlockSpec((places, rank, share), lambda i: (i, 0, 0)),
        ],
        out_specs=pl.BlockSpec(packed_shape, lambda i: (0, 0, 0)),
        scratch_shapes=[pltpu.VMEM((nights * intervals + rank, rank), jnp.float32)],
        compiler_params=STREAM,
    )(x2, full)
    send, raw, gram_a, scale = call(
        functools.partial(night_body, meters * copies),
        (
            f32(night_devices, nights + intervals // 2, 2 * rank),
            f32(nights, rank), f32(rank, rank), f32(rank, 1),
        ),
        exchange(packed, GRP), gram_c, spans.T,
    )
    evenings_out, spans_out = call(
        functools.partial(span_body, nights * night_devices),
        (f32(nights, rank), f32(intervals, rank)),
        exchange(send, NIGHT), raw, gram_a,
    )
    return own_raw / scale, evenings_out.T, spans_out.T


def solution(mesh):
    fine = Mesh(
        np.asarray(mesh.devices).reshape(tuple(SPLIT.values())), tuple(SPLIT)
    )
    in_specs = (P(NIGHT, None, GRP), P(None, NIGHT), P())
    out_specs = (P(None, GRP + NIGHT), P(None, NIGHT), P())
    return jax.shard_map(
        on_device, mesh=fine, in_specs=in_specs, out_specs=out_specs, check_vma=False
    )
```

```python
import functools

import jax
import jax.numpy as jnp
import numpy as np
from jax import lax
from jax.experimental import pallas as pl
from jax.experimental.pallas import tpu as pltpu
from jax.sharding import Mesh, PartitionSpec as P

FULL = lax.Precision.HIGHEST
EPS = 1e-06
GRP = ("ylo", "core")
NIGHT = ("x", "yhi", "z")
ZY = ("z", "yhi")
SPLIT = {"ylo": 4, "core": 2, "x": 4, "yhi": 2, "z": 8}
VMEM = pl.BlockSpec(memory_space=pltpu.VMEM)
STREAM = pltpu.CompilerParams(vmem_limit_bytes=60 * 1024 * 1024)
PARAMS = pltpu.CompilerParams(vmem_limit_bytes=40 * 1024 * 1024)


def f32(*shape):
    return jax.ShapeDtypeStruct(shape, jnp.float32)


def call(body, outs, *operands):
    return pl.pallas_call(
        body,
        out_shape=outs,
        in_specs=[VMEM] * len(operands),
        out_specs=jax.tree.map(lambda _: VMEM, outs),
        compiler_params=PARAMS,
    )(*operands)


def partial_body(nyhi, nz, nights_ref, spans_ref, x_ref, out_ref):
    rank, nights = nights_ref.shape
    intervals = spans_ref.shape[1]
    share = x_ref.shape[1] // (nyhi * nz)
    kron = jnp.dot(
        nights_ref[...], onehot(nights, nights * intervals, lambda j, c: c // intervals == j),
        precision=FULL, preferred_element_type=jnp.float32,
    ) * jnp.dot(
        spans_ref[...], onehot(intervals, nights * intervals, lambda k, c: c % intervals == k),
        precision=FULL, preferred_element_type=jnp.float32,
    )
    for y in range(nyhi):
        product = jnp.dot(
            kron, x_ref[:, y * nz * share : (y + 1) * nz * share], precision=FULL,
            preferred_element_type=jnp.float32,
        )
        for z in range(nz):
            out_ref[0, z * nyhi + y] = product[:, z * share : (z + 1) * share]


def inverse_body(gram_b_ref, gram_c_ref, out_ref):
    gram = gram_b_ref[...] * gram_c_ref[...]
    out_ref[...] = right_divide(gram, identity(gram.shape[0]))


def join_body(got_ref, gram_ref, out_ref, gram_out_ref):
    for n in range(out_ref.shape[0]):
        block = got_ref[0, n]
        for i in range(1, got_ref.shape[0]):
            block += got_ref[i, n]
        out_ref[n] = block
    gram_out_ref[...] = gram_ref[...]


def own_body(got_ref, gram_ref, own_ref, send_ref, gram_out_ref):
    products = got_ref[0]
    for i in range(1, got_ref.shape[0]):
        products += got_ref[i]
    own_ref[...] = products
    for i in range(send_ref.shape[0]):
        send_ref[i] = products
    gram_out_ref[...] = gram_ref[...]


def apply_body(inverse_ref, own_ref, got_ref, own_out_ref, send_ref):
    dot = functools.partial(jnp.dot, precision=FULL, preferred_element_type=jnp.float32)
    inverse = inverse_ref[...]
    own_out_ref[...] = dot(inverse, own_ref[...])
    step = min(8, got_ref.shape[0])
    width = got_ref.shape[-1]
    for first in range(0, got_ref.shape[0], step):
        products = jnp.concatenate([got_ref[first + i] for i in range(step)], axis=1)
        loadings = dot(inverse, products)
        for i in range(step):
            block = loadings[:, i * width : (i + 1) * width]
            for k in range(send_ref.shape[0]):
                send_ref[k, first + i] = block


def onehot(rows, columns, test):
    return test(
        lax.broadcasted_iota(jnp.int32, (rows, columns), 0),
        lax.broadcasted_iota(jnp.int32, (rows, columns), 1),
    ).astype(jnp.float32)


def identity(size):
    return onehot(size, size, lambda i, j: i == j)


def contract_body(nyhi, nz, x_ref, a_ref, out_ref):
    rank, share = a_ref.shape[1:]
    rows = x_ref.shape[0]
    total = jnp.zeros((rows + rank, rank), jnp.float32)
    for group in range(a_ref.shape[0] // nz):
        x, y = group // nyhi, group % nyhi
        loadings = jnp.concatenate(
            [a_ref[(x * nz + z) * nyhi + y] for z in range(nz)], axis=1
        )
        left = jnp.concatenate(
            [x_ref[:, group * nz * share : (group + 1) * nz * share], loadings], axis=0
        )
        total += lax.dot_general(
            left, loadings, (((1,), (1,)), ((), ())), precision=FULL,
            preferred_element_type=jnp.float32,
        )
    half, quarter = rows // 2, rank // 2
    packed = jnp.concatenate(
        [
            jnp.concatenate([total[:half], total[half:rows]], axis=1),
            jnp.concatenate([total[rows : rows + quarter], total[rows + quarter :]], axis=1),
        ],
        axis=0,
    )
    for i in range(out_ref.shape[0]):
        out_ref[i] = packed


def right_divide(gram, right):
    size = gram.shape[0]
    work = jnp.concatenate([gram, right], axis=0)
    lane = lax.broadcasted_iota(jnp.int32, (1, size), 1)
    for p in range(size):
        at = p % 8
        row = work[at : at + 1, :]
        here = lane == p
        factor = jnp.where(here, -1.0, row) / row[:, p : p + 1]
        work = jnp.where(here, 0.0, work) - work[:, p : p + 1] * factor
        if at == 7:
            work = work[8:]
    return work


def diagonals(gram):
    size = gram.shape[0]
    mask = lax.broadcasted_iota(jnp.int32, (size, size), 0) == lax.broadcasted_iota(
        jnp.int32, (size, size), 1
    )
    kept = jnp.where(mask, gram, 0.0)
    return jnp.sum(kept, axis=0, keepdims=True), jnp.sum(kept, axis=1, keepdims=True)


def night_body(
    meters, got_ref, gram_c_ref, spans_t_ref, own_ref, send_ref, raw_ref, gram_ref, columns_ref
):
    rank = gram_c_ref.shape[0]
    intervals = spans_t_ref.shape[0]
    got = got_ref[0]
    for i in range(1, got_ref.shape[0]):
        got += got_ref[i]
    half = got.shape[0] - rank // 2
    contracted = jnp.concatenate([got[:half, :rank], got[:half, rank:]], axis=0)
    gram = jnp.concatenate([got[half:, :rank], got[half:, rank:]], axis=0)
    along, down = diagonals(gram)
    along = jnp.sqrt(along / meters + EPS)
    down = jnp.sqrt(down / meters + EPS)
    gram = gram / down / along
    contracted = (contracted / along).reshape(-1, intervals, rank)
    products = jnp.sum(contracted * spans_t_ref[...][None], axis=1)
    raw = right_divide(gram * gram_c_ref[...], products)
    interval = contracted[0] * raw[0:1]
    for j in range(1, raw.shape[0]):
        interval += contracted[j] * raw[j : j + 1]
    packed = jnp.concatenate(
        [
            jnp.concatenate([raw, raw], axis=1),
            jnp.concatenate([interval[: intervals // 2], interval[intervals // 2 :]], axis=1),
        ],
        axis=0,
    )
    for i in range(send_ref.shape[0]):
        send_ref[i] = packed
    raw_ref[...] = raw
    gram_ref[...] = gram
    columns_ref[...] = own_ref[...] / down


def span_body(night_total, got_ref, raw_ref, gram_ref, evenings_ref, spans_ref):
    rank = gram_ref.shape[0]
    nights = raw_ref.shape[0]
    everything = got_ref[:, :nights, :][:, :, :rank].reshape(-1, rank)
    gram = lax.dot_general(
        everything, everything, (((0,), (0,)), ((), ())), precision=FULL,
        preferred_element_type=jnp.float32,
    )
    interval = jnp.sum(got_ref[:, nights:, :], axis=0)
    along, down = diagonals(gram)
    along = jnp.sqrt(along / night_total + EPS)
    down = jnp.sqrt(down / night_total + EPS)
    gram = gram / down / along
    interval = jnp.concatenate([interval[:, :rank], interval[:, rank:]], axis=0) / along
    raw = right_divide(gram * gram_ref[...], interval)
    scale = jnp.sqrt(jnp.mean(raw * raw, axis=0, keepdims=True) + EPS)
    evenings_ref[...] = raw_ref[...] / along
    spans_ref[...] = raw / scale


def exchange(blocks, axis):
    return lax.all_to_all(blocks, axis, 0, 0, tiled=True)


def butterfly(total, axis):
    size = lax.axis_size(axis)
    step = 1
    while step < size:
        total += lax.ppermute(total, axis, [(i, i ^ step) for i in range(size)])
        step *= 2
    return total


def on_device(readings, evenings, spans):
    rank, nights = evenings.shape
    _, intervals, meters = readings.shape
    nx, nyhi, nz = (lax.axis_size(a) for a in NIGHT)
    night_devices = nx * nyhi * nz
    share = meters // night_devices
    copies = lax.axis_size(GRP)
    x2 = readings.reshape(nights * intervals, meters)
    gram_c = jnp.dot(spans, spans.T, precision=FULL)
    places = nyhi * nz
    blocks = pl.pallas_call(
        functools.partial(partial_body, nyhi, nz),
        out_shape=f32(nx, places, rank, share),
        grid=(nx,),
        in_specs=[
            pl.BlockSpec((rank, nights), lambda i: (0, 0)),
            pl.BlockSpec((rank, intervals), lambda i: (0, 0)),
            pl.BlockSpec((nights * intervals, places * share), lambda i: (0, i)),
        ],
        out_specs=pl.BlockSpec((1, places, rank, share), lambda i: (i, 0, 0, 0)),
        compiler_params=STREAM,
    )(evenings, spans, x2)

    square = f32(rank, rank)
    gram_b = jnp.dot(evenings, evenings.T, precision=FULL)
    gram_b = butterfly(gram_b, "z")
    joined, gram_b = call(
        join_body, (f32(places, rank, share), square), exchange(blocks, "x"), gram_b
    )
    gram_b = butterfly(gram_b, "yhi")
    own, send, gram_b = call(
        own_body, (f32(rank, share), f32(places, rank, share), square),
        exchange(joined, ZY), gram_b,
    )
    gram_b = butterfly(gram_b, "x")
    inverse = call(inverse_body, square, gram_b, gram_c)
    own_raw, send = call(
        apply_body, (f32(rank, share), f32(nx, places, rank, share)),
        inverse, own, exchange(send, ZY),
    )
    full = exchange(send, "x").reshape(night_devices, rank, share)

    packed = call(
        functools.partial(contract_body, nyhi, nz),
        f32(copies, (nights * intervals + rank) // 2, 2 * rank), x2, full,
    )
    send, raw, gram_a, own_columns = call(
        functools.partial(night_body, meters * copies),
        (
            f32(night_devices, nights + intervals // 2, 2 * rank),
            f32(nights, rank), square, f32(rank, share),
        ),
        exchange(packed, GRP), gram_c, spans.T, own_raw,
    )
    evenings_out, spans_out = call(
        functools.partial(span_body, nights * night_devices),
        (f32(nights, rank), f32(intervals, rank)),
        exchange(send, NIGHT), raw, gram_a,
    )
    return own_columns, evenings_out.T, spans_out.T


def solution(mesh):
    fine = Mesh(
        np.asarray(mesh.devices).reshape(tuple(SPLIT.values())), tuple(SPLIT)
    )
    in_specs = (P(NIGHT, None, GRP), P(None, NIGHT), P())
    out_specs = (P(None, GRP + NIGHT), P(None, NIGHT), P())
    return jax.shard_map(
        on_device, mesh=fine, in_specs=in_specs, out_specs=out_specs, check_vma=False
    )
```

```python
import functools

import jax
import jax.numpy as jnp
import numpy as np
from jax import lax
from jax.experimental import pallas as pl
from jax.experimental.pallas import tpu as pltpu
from jax.sharding import Mesh, PartitionSpec as P

FULL = lax.Precision.HIGHEST
EPS = 1e-06
GRP = ("ylo", "core")
NIGHT = ("x", "yhi", "z")
ZY = ("z", "yhi")
SPLIT = {"ylo": 4, "core": 2, "x": 4, "yhi": 2, "z": 8}
VMEM = pl.BlockSpec(memory_space=pltpu.VMEM)
STREAM = pltpu.CompilerParams(vmem_limit_bytes=60 * 1024 * 1024)
FAN = pltpu.CompilerParams(vmem_limit_bytes=52 * 1024 * 1024)
CONTRACT = pltpu.CompilerParams(vmem_limit_bytes=50 * 1024 * 1024)
PARAMS = pltpu.CompilerParams(vmem_limit_bytes=40 * 1024 * 1024)


def f32(*shape):
    return jax.ShapeDtypeStruct(shape, jnp.float32)


def call(body, outs, *operands, params=PARAMS):
    return pl.pallas_call(
        body,
        out_shape=outs,
        in_specs=[VMEM] * len(operands),
        out_specs=jax.tree.map(lambda _: VMEM, outs),
        compiler_params=params,
    )(*operands)


def transposed_dot(left, right):
    return lax.dot_general(
        left, right, (((0,), (0,)), ((), ())), precision=FULL,
        preferred_element_type=jnp.float32,
    )


def partial_body(nyhi, nz, nights_ref, spans_ref, x_ref, out_ref, kron_ref):
    nights, intervals = nights_ref.shape[0], spans_ref.shape[0]
    share = x_ref.shape[1] // (nyhi * nz)

    @pl.when(pl.program_id(0) == 0)
    def _():
        columns = nights * intervals
        kron_ref[...] = transposed_dot(
            nights_ref[...], onehot(nights, columns, lambda j, c: c // intervals == j)
        ) * transposed_dot(
            spans_ref[...], onehot(intervals, columns, lambda k, c: c % intervals == k)
        )

    for y in range(nyhi):
        product = jnp.dot(
            kron_ref[...], x_ref[:, y * nz * share : (y + 1) * nz * share], precision=FULL,
            preferred_element_type=jnp.float32,
        )
        for z in range(nz):
            out_ref[0, z * nyhi + y] = product[:, z * share : (z + 1) * share]


def inverse_body(gram_b_ref, gram_c_ref, out_ref):
    gram = gram_b_ref[...] * gram_c_ref[...]
    out_ref[...] = right_divide(gram, identity(gram.shape[0]))


def join_body(got_ref, gram_ref, out_ref, gram_out_ref):
    for n in range(out_ref.shape[0]):
        block = got_ref[0, n]
        for i in range(1, got_ref.shape[0]):
            block += got_ref[i, n]
        out_ref[n] = block
    gram_out_ref[...] = gram_ref[...]


def own_body(got_ref, gram_ref, own_ref, send_ref, gram_out_ref):
    products = got_ref[0]
    for i in range(1, got_ref.shape[0]):
        products += got_ref[i]
    own_ref[...] = products
    for i in range(send_ref.shape[0]):
        send_ref[i] = products
    gram_out_ref[...] = gram_ref[...]


def fan_body(got_ref, gram_ref, send_ref, gram_out_ref):
    for k in range(send_ref.shape[0]):
        send_ref[k] = got_ref[...]
    gram_out_ref[...] = gram_ref[...]


def onehot(rows, columns, test):
    return test(
        lax.broadcasted_iota(jnp.int32, (rows, columns), 0),
        lax.broadcasted_iota(jnp.int32, (rows, columns), 1),
    ).astype(jnp.float32)


def identity(size):
    return onehot(size, size, lambda i, j: i == j)


def contract_body(
    nyhi, nz, inverse_ref, own_ref, x_ref, m_ref, out_ref, own_out_ref, held_ref, sems
):
    rank, share = m_ref.shape[1:]
    rows = x_ref.shape[0]
    copies = [
        pltpu.make_async_copy(
            x_ref.at[:, pl.ds(group * nz * share, nz * share)], held_ref.at[group], sems.at[group]
        )
        for group in range(held_ref.shape[0])
    ]
    for copy in copies:
        copy.start()
    dot = functools.partial(jnp.dot, precision=FULL, preferred_element_type=jnp.float32)
    inverse = inverse_ref[...]
    own_out_ref[...] = dot(inverse, own_ref[...])
    total = jnp.zeros((rows + rank, rank), jnp.float32)
    for group in range(held_ref.shape[0]):
        x, y = group // nyhi, group % nyhi
        products = jnp.concatenate(
            [m_ref[(x * nz + z) * nyhi + y] for z in range(nz)], axis=1
        )
        loadings = dot(inverse, products)
        copies[group].wait()
        left = jnp.concatenate([held_ref[group], loadings], axis=0)
        total += lax.dot_general(
            left, loadings, (((1,), (1,)), ((), ())), precision=FULL,
            preferred_element_type=jnp.float32,
        )
    half, quarter = rows // 2, rank // 2
    packed = jnp.concatenate(
        [
            jnp.concatenate([total[:half], total[half:rows]], axis=1),
            jnp.concatenate([total[rows : rows + quarter], total[rows + quarter :]], axis=1),
        ],
        axis=0,
    )
    for i in range(out_ref.shape[0]):
        out_ref[i] = packed


def right_divide(gram, right):
    size = gram.shape[0]
    work = jnp.concatenate([gram, right], axis=0)
    lane = lax.broadcasted_iota(jnp.int32, (1, size), 1)
    for p in range(0, size, 2):
        at, q = p % 8, p + 1
        first, second = work[at : at + 1, :], work[at + 1 : at + 2, :]
        cross = first[:, q : q + 1]
        invert = 1.0 / first[:, p : p + 1]
        ratio = cross * invert
        schur = 1.0 / (second[:, q : q + 1] - cross * ratio)
        here = (lane == p) | (lane == q)
        first = jnp.where(here, jnp.where(lane == p, -1.0, 0.0), first)
        second = jnp.where(here, jnp.where(lane == q, -1.0, 0.0), second)
        second = (second - ratio * first) * schur
        first = first * invert - ratio * second
        work = (
            jnp.where(here, 0.0, work)
            - work[:, p : p + 1] * first
            - work[:, q : q + 1] * second
        )
        if at == 6:
            work = work[8:]
    return work


def diagonals(gram):
    size = gram.shape[0]
    mask = lax.broadcasted_iota(jnp.int32, (size, size), 0) == lax.broadcasted_iota(
        jnp.int32, (size, size), 1
    )
    kept = jnp.where(mask, gram, 0.0)
    return jnp.sum(kept, axis=0, keepdims=True), jnp.sum(kept, axis=1, keepdims=True)


def night_body(
    meters, got_ref, gram_c_ref, spans_t_ref, own_ref, send_ref, raw_ref, gram_ref, columns_ref
):
    rank = gram_c_ref.shape[0]
    intervals = spans_t_ref.shape[0]
    got = got_ref[0]
    for i in range(1, got_ref.shape[0]):
        got += got_ref[i]
    half = got.shape[0] - rank // 2
    contracted = jnp.concatenate([got[:half, :rank], got[:half, rank:]], axis=0)
    gram = jnp.concatenate([got[half:, :rank], got[half:, rank:]], axis=0)
    along, down = diagonals(gram)
    along = jnp.sqrt(along / meters + EPS)
    down = jnp.sqrt(down / meters + EPS)
    gram = gram / down / along
    contracted = (contracted / along).reshape(-1, intervals, rank)
    products = jnp.sum(contracted * spans_t_ref[...][None], axis=1)
    raw = right_divide(gram * gram_c_ref[...], products)
    interval = contracted[0] * raw[0:1]
    for j in range(1, raw.shape[0]):
        interval += contracted[j] * raw[j : j + 1]
    packed = jnp.concatenate(
        [
            jnp.concatenate([raw, raw], axis=1),
            jnp.concatenate([interval[: intervals // 2], interval[intervals // 2 :]], axis=1),
        ],
        axis=0,
    )
    for i in range(send_ref.shape[0]):
        send_ref[i] = packed
    raw_ref[...] = raw
    gram_ref[...] = gram
    columns_ref[...] = own_ref[...] / down


def span_body(night_total, got_ref, raw_ref, gram_ref, evenings_ref, spans_ref):
    rank = gram_ref.shape[0]
    nights = raw_ref.shape[0]
    everything = got_ref[:, :nights, :][:, :, :rank].reshape(-1, rank)
    gram = lax.dot_general(
        everything, everything, (((0,), (0,)), ((), ())), precision=FULL,
        preferred_element_type=jnp.float32,
    )
    interval = jnp.sum(got_ref[:, nights:, :], axis=0)
    along, down = diagonals(gram)
    along = jnp.sqrt(along / night_total + EPS)
    down = jnp.sqrt(down / night_total + EPS)
    gram = gram / down / along
    interval = jnp.concatenate([interval[:, :rank], interval[:, rank:]], axis=0) / along
    raw = right_divide(gram * gram_ref[...], interval)
    scale = jnp.sqrt(jnp.mean(raw * raw, axis=0, keepdims=True) + EPS)
    evenings_ref[...] = raw_ref[...] / along
    spans_ref[...] = raw / scale


def exchange(blocks, axis):
    return lax.all_to_all(blocks, axis, 0, 0, tiled=True)


def butterfly(total, axis):
    size = lax.axis_size(axis)
    step = 1
    while step < size:
        total += lax.ppermute(total, axis, [(i, i ^ step) for i in range(size)])
        step *= 2
    return total


def on_device(readings, evenings, spans):
    rank, nights = evenings.shape
    _, intervals, meters = readings.shape
    nx, nyhi, nz = (lax.axis_size(a) for a in NIGHT)
    night_devices = nx * nyhi * nz
    share = meters // night_devices
    copies = lax.axis_size(GRP)
    x2 = readings.reshape(nights * intervals, meters)
    gram_c = jnp.dot(spans, spans.T, precision=FULL)
    places = nyhi * nz
    blocks = pl.pallas_call(
        functools.partial(partial_body, nyhi, nz),
        out_shape=f32(nx, places, rank, share),
        grid=(nx,),
        in_specs=[
            pl.BlockSpec((nights, rank), lambda i: (0, 0)),
            pl.BlockSpec((intervals, rank), lambda i: (0, 0)),
            pl.BlockSpec((nights * intervals, places * share), lambda i: (0, i)),
        ],
        out_specs=pl.BlockSpec((1, places, rank, share), lambda i: (i, 0, 0, 0)),
        scratch_shapes=[pltpu.VMEM((rank, nights * intervals), jnp.float32)],
        compiler_params=STREAM,
    )(evenings.T, spans.T, x2)

    square = f32(rank, rank)
    gram_b = jnp.dot(evenings, evenings.T, precision=FULL)
    gram_b = butterfly(gram_b, "z")
    joined, gram_b = call(
        join_body, (f32(places, rank, share), square), exchange(blocks, "x"), gram_b
    )
    gram_b = butterfly(gram_b, "x")
    own, send, gram_b = call(
        own_body, (f32(rank, share), f32(places, rank, share), square),
        exchange(joined, ZY), gram_b,
    )
    send, gram_b = call(
        fan_body, (f32(nx, places, rank, share), square), exchange(send, ZY), gram_b,
        params=FAN,
    )
    gram_b = butterfly(gram_b, "yhi")
    inverse = call(inverse_body, square, gram_b, gram_c)
    full = exchange(send, "x").reshape(night_devices, rank, share)

    groups = nx * nyhi
    packed, own_raw = pl.pallas_call(
        functools.partial(contract_body, nyhi, nz),
        out_shape=(f32(copies, (nights * intervals + rank) // 2, 2 * rank), f32(rank, share)),
        in_specs=[VMEM, VMEM, pl.BlockSpec(memory_space=pl.ANY), VMEM],
        out_specs=(VMEM, VMEM),
        scratch_shapes=[
            pltpu.VMEM((groups, nights * intervals, nz * share), jnp.float32),
            pltpu.SemaphoreType.DMA((groups,)),
        ],
        compiler_params=CONTRACT,
    )(inverse, own, x2, full)
    send, raw, gram_a, own_columns = call(
        functools.partial(night_body, meters * copies),
        (
            f32(night_devices, nights + intervals // 2, 2 * rank),
            f32(nights, rank), square, f32(rank, share),
        ),
        exchange(packed, GRP), gram_c, spans.T, own_raw,
    )
    evenings_out, spans_out = call(
        functools.partial(span_body, nights * night_devices),
        (f32(nights, rank), f32(intervals, rank)),
        exchange(send, NIGHT), raw, gram_a,
    )
    return own_columns, evenings_out.T, spans_out.T


def solution(mesh):
    fine = Mesh(
        np.asarray(mesh.devices).reshape(tuple(SPLIT.values())), tuple(SPLIT)
    )
    in_specs = (P(NIGHT, None, GRP), P(None, NIGHT), P())
    out_specs = (P(None, GRP + NIGHT), P(None, NIGHT), P())
    return jax.shard_map(
        on_device, mesh=fine, in_specs=in_specs, out_specs=out_specs, check_vma=False
    )
```

```python
import functools

import jax
import jax.numpy as jnp
import numpy as np
from jax import lax
from jax.experimental import pallas as pl
from jax.experimental.pallas import tpu as pltpu
from jax.sharding import Mesh, PartitionSpec as P

FULL = lax.Precision.HIGHEST
EPS = 1e-06
GRP = ("ylo", "core")
NIGHT = ("x", "yhi", "z")
ZY = ("z", "yhi")
SPLIT = {"ylo": 4, "core": 2, "x": 4, "yhi": 2, "z": 8}
VMEM = pl.BlockSpec(memory_space=pltpu.VMEM)
STREAM = pltpu.CompilerParams(vmem_limit_bytes=60 * 1024 * 1024)
FAN = pltpu.CompilerParams(vmem_limit_bytes=52 * 1024 * 1024)
CONTRACT = pltpu.CompilerParams(vmem_limit_bytes=50 * 1024 * 1024)
PARAMS = pltpu.CompilerParams(vmem_limit_bytes=40 * 1024 * 1024)


def f32(*shape):
    return jax.ShapeDtypeStruct(shape, jnp.float32)


def call(body, outs, *operands, params=PARAMS):
    return pl.pallas_call(
        body,
        out_shape=outs,
        in_specs=[VMEM] * len(operands),
        out_specs=jax.tree.map(lambda _: VMEM, outs),
        compiler_params=params,
    )(*operands)


def split(values):
    high = values.astype(jnp.bfloat16)
    return high, (values - high.astype(jnp.float32)).astype(jnp.bfloat16)


def transposed_dot(left, right):
    return lax.dot_general(
        left, right, (((0,), (0,)), ((), ())), precision=FULL,
        preferred_element_type=jnp.float32,
    )


def partial_body(nyhi, nz, nights_ref, spans_ref, x_ref, out_ref, kron_ref):
    nights, intervals = nights_ref.shape[0], spans_ref.shape[0]
    share = x_ref.shape[1] // (nyhi * nz)

    @pl.when(pl.program_id(0) == 0)
    def _():
        columns = nights * intervals
        kron_ref[...] = transposed_dot(
            nights_ref[...], onehot(nights, columns, lambda j, c: c // intervals == j)
        ) * transposed_dot(
            spans_ref[...], onehot(intervals, columns, lambda k, c: c % intervals == k)
        )

    high, low = split(kron_ref[...])
    rank = kron_ref.shape[0]
    left = jnp.concatenate(
        [
            jnp.concatenate([high, high], axis=1),
            jnp.concatenate([low, jnp.zeros_like(low)], axis=1),
        ],
        axis=0,
    )
    for y in range(nyhi):
        right = jnp.concatenate(
            split(x_ref[:, y * nz * share : (y + 1) * nz * share]), axis=0
        )
        product = jnp.dot(left, right, preferred_element_type=jnp.float32)
        product = product[:rank] + product[rank:]
        for z in range(nz):
            out_ref[0, z * nyhi + y] = product[:, z * share : (z + 1) * share]


def inverse_body(gram_b_ref, gram_c_ref, out_ref):
    gram = gram_b_ref[...] * gram_c_ref[...]
    out_ref[...] = right_divide(gram, identity(gram.shape[0]))


def join_body(got_ref, gram_ref, out_ref, gram_out_ref):
    for n in range(out_ref.shape[0]):
        block = got_ref[0, n]
        for i in range(1, got_ref.shape[0]):
            block += got_ref[i, n]
        out_ref[n] = block
    gram_out_ref[...] = gram_ref[...]


def own_body(got_ref, gram_ref, own_ref, send_ref, gram_out_ref):
    products = got_ref[0]
    for i in range(1, got_ref.shape[0]):
        products += got_ref[i]
    own_ref[...] = products
    for i in range(send_ref.shape[0]):
        send_ref[i] = products
    gram_out_ref[...] = gram_ref[...]


def fan_body(got_ref, gram_ref, send_ref, gram_out_ref):
    for k in range(send_ref.shape[0]):
        send_ref[k] = got_ref[...]
    gram_out_ref[...] = gram_ref[...]


def onehot(rows, columns, test):
    return test(
        lax.broadcasted_iota(jnp.int32, (rows, columns), 0),
        lax.broadcasted_iota(jnp.int32, (rows, columns), 1),
    ).astype(jnp.float32)


def identity(size):
    return onehot(size, size, lambda i, j: i == j)


def contract_body(
    nyhi, nz, inverse_ref, own_ref, x_ref, m_ref, out_ref, own_out_ref, held_ref, sems
):
    rank, share = m_ref.shape[1:]
    rows = x_ref.shape[0]
    copies = [
        pltpu.make_async_copy(
            x_ref.at[:, pl.ds(group * nz * share, nz * share)], held_ref.at[group], sems.at[group]
        )
        for group in range(held_ref.shape[0])
    ]
    for copy in copies:
        copy.start()
    inverse = inverse_ref[...]
    own_out_ref[...] = jnp.dot(
        inverse, own_ref[...], precision=FULL, preferred_element_type=jnp.float32
    )
    high, low = split(inverse)
    solver = jnp.concatenate([high, high, low], axis=1)
    loadings = []
    for group in range(held_ref.shape[0]):
        x, y = group // nyhi, group % nyhi
        high, low = split(
            jnp.concatenate([m_ref[(x * nz + z) * nyhi + y] for z in range(nz)], axis=1)
        )
        factor = jnp.dot(
            solver, jnp.concatenate([high, low, high], axis=0),
            preferred_element_type=jnp.float32,
        )
        loadings.append(split(factor))
    total = jnp.zeros((2 * (rows + rank), 2 * rank), jnp.float32)
    for group, (high, low) in enumerate(loadings):
        copies[group].wait()
        x_high, x_low = split(held_ref[group])
        total += lax.dot_general(
            jnp.concatenate([x_high, high, x_low, low], axis=0),
            jnp.concatenate([high, low], axis=0),
            (((1,), (1,)), ((), ())), preferred_element_type=jnp.float32,
        )
    total = total[:, :rank] + total[:, rank:]
    total = total[: rows + rank] + total[rows + rank :]
    half, quarter = rows // 2, rank // 2
    packed = jnp.concatenate(
        [
            jnp.concatenate([total[:half], total[half:rows]], axis=1),
            jnp.concatenate([total[rows : rows + quarter], total[rows + quarter :]], axis=1),
        ],
        axis=0,
    )
    for i in range(out_ref.shape[0]):
        out_ref[i] = packed


def right_divide(gram, right):
    size = gram.shape[0]
    work = jnp.concatenate([gram, right], axis=0)
    lane = lax.broadcasted_iota(jnp.int32, (1, size), 1)
    for p in range(size):
        at = p % 8
        row = work[at : at + 1, :]
        here = lane == p
        factor = jnp.where(here, -1.0, row) / row[:, p : p + 1]
        work = jnp.where(here, 0.0, work) - work[:, p : p + 1] * factor
        if at == 7:
            work = work[8:]
    return work


def diagonals(gram):
    size = gram.shape[0]
    mask = lax.broadcasted_iota(jnp.int32, (size, size), 0) == lax.broadcasted_iota(
        jnp.int32, (size, size), 1
    )
    kept = jnp.where(mask, gram, 0.0)
    return jnp.sum(kept, axis=0, keepdims=True), jnp.sum(kept, axis=1, keepdims=True)


def night_body(
    meters, got_ref, gram_c_ref, spans_t_ref, own_ref, send_ref, raw_ref, gram_ref, columns_ref
):
    rank = gram_c_ref.shape[0]
    intervals = spans_t_ref.shape[0]
    got = got_ref[0]
    for i in range(1, got_ref.shape[0]):
        got += got_ref[i]
    half = got.shape[0] - rank // 2
    contracted = jnp.concatenate([got[:half, :rank], got[:half, rank:]], axis=0)
    gram = jnp.concatenate([got[half:, :rank], got[half:, rank:]], axis=0)
    along, down = diagonals(gram)
    along = jnp.sqrt(along / meters + EPS)
    down = jnp.sqrt(down / meters + EPS)
    gram = gram / down / along
    contracted = (contracted / along).reshape(-1, intervals, rank)
    products = jnp.sum(contracted * spans_t_ref[...][None], axis=1)
    raw = right_divide(gram * gram_c_ref[...], products)
    interval = contracted[0] * raw[0:1]
    for j in range(1, raw.shape[0]):
        interval += contracted[j] * raw[j : j + 1]
    packed = jnp.concatenate(
        [
            jnp.concatenate([raw, raw], axis=1),
            jnp.concatenate([interval[: intervals // 2], interval[intervals // 2 :]], axis=1),
        ],
        axis=0,
    )
    for i in range(send_ref.shape[0]):
        send_ref[i] = packed
    raw_ref[...] = raw
    gram_ref[...] = gram
    columns_ref[...] = own_ref[...] / down


def span_body(night_total, got_ref, raw_ref, gram_ref, evenings_ref, spans_ref):
    rank = gram_ref.shape[0]
    nights = raw_ref.shape[0]
    everything = got_ref[:, :nights, :][:, :, :rank].reshape(-1, rank)
    gram = lax.dot_general(
        everything, everything, (((0,), (0,)), ((), ())), precision=FULL,
        preferred_element_type=jnp.float32,
    )
    interval = jnp.sum(got_ref[:, nights:, :], axis=0)
    along, down = diagonals(gram)
    along = jnp.sqrt(along / night_total + EPS)
    down = jnp.sqrt(down / night_total + EPS)
    gram = gram / down / along
    interval = jnp.concatenate([interval[:, :rank], interval[:, rank:]], axis=0) / along
    raw = right_divide(gram * gram_ref[...], interval)
    scale = jnp.sqrt(jnp.mean(raw * raw, axis=0, keepdims=True) + EPS)
    evenings_ref[...] = raw_ref[...] / along
    spans_ref[...] = raw / scale


def exchange(blocks, axis):
    return lax.all_to_all(blocks, axis, 0, 0, tiled=True)


def butterfly(total, axis):
    size = lax.axis_size(axis)
    step = 1
    while step < size:
        total += lax.ppermute(total, axis, [(i, i ^ step) for i in range(size)])
        step *= 2
    return total


def on_device(readings, evenings, spans):
    rank, nights = evenings.shape
    _, intervals, meters = readings.shape
    nx, nyhi, nz = (lax.axis_size(a) for a in NIGHT)
    night_devices = nx * nyhi * nz
    share = meters // night_devices
    copies = lax.axis_size(GRP)
    x2 = readings.reshape(nights * intervals, meters)
    gram_c = jnp.dot(spans, spans.T, precision=FULL)
    places = nyhi * nz
    blocks = pl.pallas_call(
        functools.partial(partial_body, nyhi, nz),
        out_shape=f32(nx, places, rank, share),
        grid=(nx,),
        in_specs=[
            pl.BlockSpec((nights, rank), lambda i: (0, 0)),
            pl.BlockSpec((intervals, rank), lambda i: (0, 0)),
            pl.BlockSpec((nights * intervals, places * share), lambda i: (0, i)),
        ],
        out_specs=pl.BlockSpec((1, places, rank, share), lambda i: (i, 0, 0, 0)),
        scratch_shapes=[pltpu.VMEM((rank, nights * intervals), jnp.float32)],
        compiler_params=STREAM,
    )(evenings.T, spans.T, x2)

    square = f32(rank, rank)
    gram_b = jnp.dot(evenings, evenings.T, precision=FULL)
    gram_b = butterfly(gram_b, "z")
    joined, gram_b = call(
        join_body, (f32(places, rank, share), square), exchange(blocks, "x"), gram_b
    )
    gram_b = butterfly(gram_b, "x")
    own, send, gram_b = call(
        own_body, (f32(rank, share), f32(places, rank, share), square),
        exchange(joined, ZY), gram_b,
    )
    send, gram_b = call(
        fan_body, (f32(nx, places, rank, share), square), exchange(send, ZY), gram_b,
        params=FAN,
    )
    gram_b = butterfly(gram_b, "yhi")
    inverse = call(inverse_body, square, gram_b, gram_c)
    full = exchange(send, "x").reshape(night_devices, rank, share)

    groups = nx * nyhi
    packed, own_raw = pl.pallas_call(
        functools.partial(contract_body, nyhi, nz),
        out_shape=(f32(copies, (nights * intervals + rank) // 2, 2 * rank), f32(rank, share)),
        in_specs=[VMEM, VMEM, pl.BlockSpec(memory_space=pl.ANY), VMEM],
        out_specs=(VMEM, VMEM),
        scratch_shapes=[
            pltpu.VMEM((groups, nights * intervals, nz * share), jnp.float32),
            pltpu.SemaphoreType.DMA((groups,)),
        ],
        compiler_params=CONTRACT,
    )(inverse, own, x2, full)
    send, raw, gram_a, own_columns = call(
        functools.partial(night_body, meters * copies),
        (
            f32(night_devices, nights + intervals // 2, 2 * rank),
            f32(nights, rank), square, f32(rank, share),
        ),
        exchange(packed, GRP), gram_c, spans.T, own_raw,
    )
    evenings_out, spans_out = call(
        functools.partial(span_body, nights * night_devices),
        (f32(nights, rank), f32(intervals, rank)),
        exchange(send, NIGHT), raw, gram_a,
    )
    return own_columns, evenings_out.T, spans_out.T


def solution(mesh):
    fine = Mesh(
        np.asarray(mesh.devices).reshape(tuple(SPLIT.values())), tuple(SPLIT)
    )
    in_specs = (P(NIGHT, None, GRP), P(None, NIGHT), P())
    out_specs = (P(None, GRP + NIGHT), P(None, NIGHT), P())
    return jax.shard_map(
        on_device, mesh=fine, in_specs=in_specs, out_specs=out_specs, check_vma=False
    )
```

```python
import functools

import jax
import jax.numpy as jnp
import numpy as np
from jax import lax
from jax.experimental import pallas as pl
from jax.experimental.pallas import tpu as pltpu
from jax.sharding import Mesh, PartitionSpec as P

FULL = lax.Precision.HIGHEST
EPS = 1e-06
GRP = ("ylo", "core")
NIGHT = ("x", "yhi", "z")
ZY = ("z", "yhi")
SPLIT = {"ylo": 4, "core": 2, "x": 4, "yhi": 2, "z": 8}
VMEM = pl.BlockSpec(memory_space=pltpu.VMEM)
STREAM = pltpu.CompilerParams(vmem_limit_bytes=60 * 1024 * 1024)
FAN = pltpu.CompilerParams(vmem_limit_bytes=52 * 1024 * 1024)
CONTRACT = pltpu.CompilerParams(vmem_limit_bytes=50 * 1024 * 1024)
PARAMS = pltpu.CompilerParams(vmem_limit_bytes=40 * 1024 * 1024)


def f32(*shape):
    return jax.ShapeDtypeStruct(shape, jnp.float32)


def call(body, outs, *operands, params=PARAMS):
    return pl.pallas_call(
        body,
        out_shape=outs,
        in_specs=[VMEM] * len(operands),
        out_specs=jax.tree.map(lambda _: VMEM, outs),
        compiler_params=params,
    )(*operands)


def split(values):
    high = values.astype(jnp.bfloat16)
    return high, (values - high.astype(jnp.float32)).astype(jnp.bfloat16)


def transposed_dot(left, right):
    return lax.dot_general(
        left, right, (((0,), (0,)), ((), ())), precision=FULL,
        preferred_element_type=jnp.float32,
    )


def partial_body(
    nyhi, nz, nights_ref, spans_ref, x_ref, out_ref, held_ref, made_ref, in_sems, out_sems
):
    nights, rank = nights_ref.shape
    intervals = spans_ref.shape[0]
    share = out_ref.shape[-1]
    groups, width = held_ref.shape[0], nz * share
    arrivals = [
        pltpu.make_async_copy(
            x_ref.at[:, pl.ds(group * width, width)], held_ref.at[group], in_sems.at[group]
        )
        for group in range(groups)
    ]
    for copy in arrivals:
        copy.start()
    columns = nights * intervals
    kron = transposed_dot(
        nights_ref[...], onehot(nights, columns, lambda j, c: c // intervals == j)
    ) * transposed_dot(
        spans_ref[...], onehot(intervals, columns, lambda k, c: c % intervals == k)
    )
    high, low = split(kron)
    left = jnp.concatenate(
        [
            jnp.concatenate([high, high], axis=1),
            jnp.concatenate([low, jnp.zeros_like(low)], axis=1),
        ],
        axis=0,
    )
    departures = []
    for group in range(groups):
        x, y = group // nyhi, group % nyhi
        arrivals[group].wait()
        right = jnp.concatenate(split(held_ref[group]), axis=0)
        product = jnp.dot(left, right, preferred_element_type=jnp.float32)
        product = product[:rank] + product[rank:]
        for z in range(nz):
            made_ref[x, z * nyhi + y] = product[:, z * share : (z + 1) * share]
        if y == nyhi - 1:
            copy = pltpu.make_async_copy(made_ref.at[x], out_ref.at[x], out_sems.at[x])
            copy.start()
            departures.append(copy)
    for copy in departures:
        copy.wait()


def inverse_body(gram_b_ref, gram_c_ref, out_ref):
    gram = gram_b_ref[...] * gram_c_ref[...]
    out_ref[...] = right_divide(gram, identity(gram.shape[0]))


def join_body(got_ref, gram_ref, out_ref, gram_out_ref):
    for n in range(out_ref.shape[0]):
        block = got_ref[0, n]
        for i in range(1, got_ref.shape[0]):
            block += got_ref[i, n]
        out_ref[n] = block
    gram_out_ref[...] = gram_ref[...]


def own_body(got_ref, gram_ref, own_ref, send_ref, gram_out_ref):
    products = got_ref[0]
    for i in range(1, got_ref.shape[0]):
        products += got_ref[i]
    own_ref[...] = products
    for i in range(send_ref.shape[0]):
        send_ref[i] = products
    gram_out_ref[...] = gram_ref[...]


def fan_body(got_ref, gram_ref, send_ref, gram_out_ref):
    for k in range(send_ref.shape[0]):
        send_ref[k] = got_ref[...]
    gram_out_ref[...] = gram_ref[...]


def onehot(rows, columns, test):
    return test(
        lax.broadcasted_iota(jnp.int32, (rows, columns), 0),
        lax.broadcasted_iota(jnp.int32, (rows, columns), 1),
    ).astype(jnp.float32)


def identity(size):
    return onehot(size, size, lambda i, j: i == j)


def contract_body(
    nyhi, nz, inverse_ref, own_ref, x_ref, m_ref, out_ref, own_out_ref, held_ref, sems
):
    rank, share = m_ref.shape[1:]
    rows = x_ref.shape[0]
    copies = [
        pltpu.make_async_copy(
            x_ref.at[:, pl.ds(group * nz * share, nz * share)], held_ref.at[group], sems.at[group]
        )
        for group in range(held_ref.shape[0])
    ]
    for copy in copies:
        copy.start()
    inverse = inverse_ref[...]
    own_out_ref[...] = jnp.dot(
        inverse, own_ref[...], precision=FULL, preferred_element_type=jnp.float32
    )
    high, low = split(inverse)
    solver = jnp.concatenate([high, high, low], axis=1)
    loadings = []
    for group in range(held_ref.shape[0]):
        x, y = group // nyhi, group % nyhi
        high, low = split(
            jnp.concatenate([m_ref[(x * nz + z) * nyhi + y] for z in range(nz)], axis=1)
        )
        factor = jnp.dot(
            solver, jnp.concatenate([high, low, high], axis=0),
            preferred_element_type=jnp.float32,
        )
        loadings.append(split(factor))
    total = jnp.zeros((2 * (rows + rank), 2 * rank), jnp.float32)
    for group, (high, low) in enumerate(loadings):
        copies[group].wait()
        x_high, x_low = split(held_ref[group])
        total += lax.dot_general(
            jnp.concatenate([x_high, high, x_low, low], axis=0),
            jnp.concatenate([high, low], axis=0),
            (((1,), (1,)), ((), ())), preferred_element_type=jnp.float32,
        )
    total = total[:, :rank] + total[:, rank:]
    total = total[: rows + rank] + total[rows + rank :]
    half, quarter = rows // 2, rank // 2
    packed = jnp.concatenate(
        [
            jnp.concatenate([total[:half], total[half:rows]], axis=1),
            jnp.concatenate([total[rows : rows + quarter], total[rows + quarter :]], axis=1),
        ],
        axis=0,
    )
    for i in range(out_ref.shape[0]):
        out_ref[i] = packed


def right_divide(gram, right):
    size, block = gram.shape[0], 8
    work = jnp.concatenate([gram, right], axis=0)
    lane = lax.broadcasted_iota(jnp.int32, (1, size), 1)
    for p in range(0, size, block):
        rows = [work[i : i + 1, :] for i in range(block)]
        d = {
            (i, j): jnp.broadcast_to(rows[i][:, p + j : p + j + 1], (1, size))
            for i in range(block)
            for j in range(i, block)
        }
        here = (lane >= p) & (lane < p + block)
        y = [
            jnp.where(here, jnp.where(lane == p + i, -1.0, 0.0), rows[i])
            for i in range(block)
        ]
        inverse, low = [], {}
        for i in range(block):
            inverse.append(1.0 / d[i, i])
            for j in range(i + 1, block):
                low[j, i] = d[i, j] * inverse[i]
            for j in range(i + 1, block):
                for k in range(j, block):
                    d[j, k] -= low[j, i] * d[i, k]
                y[j] -= low[j, i] * y[i]
        factors = [None] * block
        for i in reversed(range(block)):
            factors[i] = y[i] * inverse[i]
            for j in range(i + 1, block):
                factors[i] -= low[j, i] * factors[j]
        rest = work[block:]
        work = jnp.where(here, 0.0, rest)
        for i in range(block):
            work -= rest[:, p + i : p + i + 1] * factors[i]
    return work


def diagonals(gram):
    size = gram.shape[0]
    mask = lax.broadcasted_iota(jnp.int32, (size, size), 0) == lax.broadcasted_iota(
        jnp.int32, (size, size), 1
    )
    kept = jnp.where(mask, gram, 0.0)
    return jnp.sum(kept, axis=0, keepdims=True), jnp.sum(kept, axis=1, keepdims=True)


def night_body(
    meters, got_ref, gram_c_ref, spans_t_ref, own_ref, send_ref, raw_ref, gram_ref, columns_ref
):
    rank = gram_c_ref.shape[0]
    intervals = spans_t_ref.shape[0]
    got = got_ref[0]
    for i in range(1, got_ref.shape[0]):
        got += got_ref[i]
    half = got.shape[0] - rank // 2
    contracted = jnp.concatenate([got[:half, :rank], got[:half, rank:]], axis=0)
    gram = jnp.concatenate([got[half:, :rank], got[half:, rank:]], axis=0)
    along, down = diagonals(gram)
    along = jnp.sqrt(along / meters + EPS)
    down = jnp.sqrt(down / meters + EPS)
    gram = gram / down / along
    contracted = (contracted / along).reshape(-1, intervals, rank)
    products = jnp.sum(contracted * spans_t_ref[...][None], axis=1)
    raw = right_divide(gram * gram_c_ref[...], products)
    interval = contracted[0] * raw[0:1]
    for j in range(1, raw.shape[0]):
        interval += contracted[j] * raw[j : j + 1]
    packed = jnp.concatenate(
        [
            jnp.concatenate([raw, raw], axis=1),
            jnp.concatenate([interval[: intervals // 2], interval[intervals // 2 :]], axis=1),
        ],
        axis=0,
    )
    for i in range(send_ref.shape[0]):
        send_ref[i] = packed
    raw_ref[...] = raw
    gram_ref[...] = gram
    columns_ref[...] = own_ref[...] / down


def span_body(night_total, got_ref, raw_ref, gram_ref, evenings_ref, spans_ref):
    rank = gram_ref.shape[0]
    nights = raw_ref.shape[0]
    everything = got_ref[:, :nights, :][:, :, :rank].reshape(-1, rank)
    gram = lax.dot_general(
        everything, everything, (((0,), (0,)), ((), ())), precision=FULL,
        preferred_element_type=jnp.float32,
    )
    interval = jnp.sum(got_ref[:, nights:, :], axis=0)
    along, down = diagonals(gram)
    along = jnp.sqrt(along / night_total + EPS)
    down = jnp.sqrt(down / night_total + EPS)
    gram = gram / down / along
    interval = jnp.concatenate([interval[:, :rank], interval[:, rank:]], axis=0) / along
    raw = right_divide(gram * gram_ref[...], interval)
    scale = jnp.sqrt(jnp.mean(raw * raw, axis=0, keepdims=True) + EPS)
    evenings_ref[...] = raw_ref[...] / along
    spans_ref[...] = raw / scale


def exchange(blocks, axis):
    return lax.all_to_all(blocks, axis, 0, 0, tiled=True)


def butterfly(total, axis):
    size = lax.axis_size(axis)
    step = 1
    while step < size:
        total += lax.ppermute(total, axis, [(i, i ^ step) for i in range(size)])
        step *= 2
    return total


def on_device(readings, evenings, spans):
    rank, nights = evenings.shape
    _, intervals, meters = readings.shape
    nx, nyhi, nz = (lax.axis_size(a) for a in NIGHT)
    night_devices = nx * nyhi * nz
    share = meters // night_devices
    copies = lax.axis_size(GRP)
    x2 = readings.reshape(nights * intervals, meters)
    gram_c = jnp.dot(spans, spans.T, precision=FULL)
    places = nyhi * nz
    groups = nx * nyhi
    anywhere = pl.BlockSpec(memory_space=pl.ANY)
    held = pltpu.VMEM((groups, nights * intervals, nz * share), jnp.float32)
    blocks = pl.pallas_call(
        functools.partial(partial_body, nyhi, nz),
        out_shape=f32(nx, places, rank, share),
        in_specs=[VMEM, VMEM, anywhere],
        out_specs=anywhere,
        scratch_shapes=[
            held,
            pltpu.VMEM((nx, places, rank, share), jnp.float32),
            pltpu.SemaphoreType.DMA((groups,)),
            pltpu.SemaphoreType.DMA((nx,)),
        ],
        compiler_params=STREAM,
    )(evenings.T, spans.T, x2)

    square = f32(rank, rank)
    gram_b = jnp.dot(evenings, evenings.T, precision=FULL)
    gram_b = butterfly(gram_b, "z")
    joined, gram_b = call(
        join_body, (f32(places, rank, share), square), exchange(blocks, "x"), gram_b
    )
    gram_b = butterfly(gram_b, "x")
    own, send, gram_b = call(
        own_body, (f32(rank, share), f32(places, rank, share), square),
        exchange(joined, ZY), gram_b,
    )
    send, gram_b = call(
        fan_body, (f32(nx, places, rank, share), square), exchange(send, ZY), gram_b,
        params=FAN,
    )
    gram_b = butterfly(gram_b, "yhi")
    inverse = call(inverse_body, square, gram_b, gram_c)
    full = exchange(send, "x").reshape(night_devices, rank, share)

    packed, own_raw = pl.pallas_call(
        functools.partial(contract_body, nyhi, nz),
        out_shape=(f32(copies, (nights * intervals + rank) // 2, 2 * rank), f32(rank, share)),
        in_specs=[VMEM, VMEM, anywhere, VMEM],
        out_specs=(VMEM, VMEM),
        scratch_shapes=[held, pltpu.SemaphoreType.DMA((groups,))],
        compiler_params=CONTRACT,
    )(inverse, own, x2, full)
    send, raw, gram_a, own_columns = call(
        functools.partial(night_body, meters * copies),
        (
            f32(night_devices, nights + intervals // 2, 2 * rank),
            f32(nights, rank), square, f32(rank, share),
        ),
        exchange(packed, GRP), gram_c, spans.T, own_raw,
    )
    evenings_out, spans_out = call(
        functools.partial(span_body, nights * night_devices),
        (f32(nights, rank), f32(intervals, rank)),
        exchange(send, NIGHT), raw, gram_a,
    )
    return own_columns, evenings_out.T, spans_out.T


def solution(mesh):
    fine = Mesh(
        np.asarray(mesh.devices).reshape(tuple(SPLIT.values())), tuple(SPLIT)
    )
    in_specs = (P(NIGHT, None, GRP), P(None, NIGHT), P())
    out_specs = (P(None, GRP + NIGHT), P(None, NIGHT), P())
    return jax.shard_map(
        on_device, mesh=fine, in_specs=in_specs, out_specs=out_specs, check_vma=False
    )
```

```python
import functools

import jax
import jax.numpy as jnp
import numpy as np
from jax import lax
from jax.experimental import pallas as pl
from jax.experimental.pallas import tpu as pltpu
from jax.sharding import Mesh, PartitionSpec as P

FULL = lax.Precision.HIGHEST
EPS = 1e-06
GRP = ("ylo", "core")
NIGHT = ("x", "yhi", "z")
ZY = ("z", "yhi")
SPLIT = {"ylo": 4, "core": 2, "x": 4, "yhi": 2, "z": 8}
VMEM = pl.BlockSpec(memory_space=pltpu.VMEM)
STREAM = pltpu.CompilerParams(vmem_limit_bytes=60 * 1024 * 1024)
CONTRACT = pltpu.CompilerParams(vmem_limit_bytes=50 * 1024 * 1024)
PARAMS = pltpu.CompilerParams(vmem_limit_bytes=40 * 1024 * 1024)


def f32(*shape):
    return jax.ShapeDtypeStruct(shape, jnp.float32)


def call(body, outs, *operands, params=PARAMS):
    return pl.pallas_call(
        body,
        out_shape=outs,
        in_specs=[VMEM] * len(operands),
        out_specs=jax.tree.map(lambda _: VMEM, outs),
        compiler_params=params,
    )(*operands)


def split(values):
    high = values.astype(jnp.bfloat16)
    return high, (values - high.astype(jnp.float32)).astype(jnp.bfloat16)


def transposed_dot(left, right):
    return lax.dot_general(
        left, right, (((0,), (0,)), ((), ())), precision=FULL,
        preferred_element_type=jnp.float32,
    )


def partial_body(
    nyhi, nz, nights_ref, spans_ref, x_ref, out_ref, held_ref, made_ref, in_sems, out_sems
):
    nights, rank = nights_ref.shape
    intervals = spans_ref.shape[0]
    share = out_ref.shape[-1]
    groups, width = held_ref.shape[0], nz * share
    arrivals = [
        pltpu.make_async_copy(
            x_ref.at[:, pl.ds(group * width, width)], held_ref.at[group], in_sems.at[group]
        )
        for group in range(groups)
    ]
    for copy in arrivals:
        copy.start()
    columns = nights * intervals
    kron = transposed_dot(
        nights_ref[...], onehot(nights, columns, lambda j, c: c // intervals == j)
    ) * transposed_dot(
        spans_ref[...], onehot(intervals, columns, lambda k, c: c % intervals == k)
    )
    high, low = split(kron)
    left = jnp.concatenate(
        [
            jnp.concatenate([high, high], axis=1),
            jnp.concatenate([low, jnp.zeros_like(low)], axis=1),
        ],
        axis=0,
    )
    departures = []
    for group in range(groups):
        x, y = group // nyhi, group % nyhi
        arrivals[group].wait()
        right = jnp.concatenate(split(held_ref[group]), axis=0)
        product = jnp.dot(left, right, preferred_element_type=jnp.float32)
        product = product[:rank] + product[rank:]
        for z in range(nz):
            made_ref[x, z * nyhi + y] = product[:, z * share : (z + 1) * share]
        if y == nyhi - 1:
            copy = pltpu.make_async_copy(made_ref.at[x], out_ref.at[x], out_sems.at[x])
            copy.start()
            departures.append(copy)
    for copy in departures:
        copy.wait()


def inverse_body(gram_b_ref, gram_c_ref, out_ref):
    gram = gram_b_ref[...] * gram_c_ref[...]
    out_ref[...] = right_divide(gram, identity(gram.shape[0]))


def join_body(got_ref, gram_ref, out_ref, gram_out_ref):
    for n in range(out_ref.shape[0]):
        block = got_ref[0, n]
        for i in range(1, got_ref.shape[0]):
            block += got_ref[i, n]
        out_ref[n] = block
    gram_out_ref[...] = gram_ref[...]


def own_body(got_ref, gram_ref, own_ref, send_ref, gram_out_ref):
    products = got_ref[0]
    for i in range(1, got_ref.shape[0]):
        products += got_ref[i]
    own_ref[...] = products
    for i in range(send_ref.shape[0]):
        send_ref[i] = products
    gram_out_ref[...] = gram_ref[...]


def relay_body(left_ref, right_ref, inverse_ref, first_ref, second_ref, inverse_out_ref):
    half = first_ref.shape[0]
    first_ref[...] = left_ref[:half]
    second_ref[...] = right_ref[half:]
    inverse_out_ref[...] = inverse_ref[...]


def onehot(rows, columns, test):
    return test(
        lax.broadcasted_iota(jnp.int32, (rows, columns), 0),
        lax.broadcasted_iota(jnp.int32, (rows, columns), 1),
    ).astype(jnp.float32)


def identity(size):
    return onehot(size, size, lambda i, j: i == j)


def contracted_blocks(nyhi, nz, place_ref, inverse, x_ref, chunks, held_ref, sems):
    nx = place_ref[1]
    rank, share = chunks[0][1][0].shape
    rows, width = held_ref.shape[1:]
    copies = []
    for distance, _ in chunks:
        x = lax.rem(place_ref[0] + distance, nx)
        for y in range(nyhi):
            start = pl.multiple_of((x * nyhi + y) * width, width)
            at = len(copies)
            copies.append(
                pltpu.make_async_copy(
                    x_ref.at[:, pl.ds(start, width)], held_ref.at[at], sems.at[at]
                )
            )
    for copy in copies:
        copy.start()
    high, low = split(inverse)
    solver = jnp.concatenate([high, high, low], axis=1)
    loadings = []
    for _, blocks in chunks:
        for y in range(nyhi):
            high, low = split(
                jnp.concatenate([blocks[z * nyhi + y] for z in range(nz)], axis=1)
            )
            factor = jnp.dot(
                solver, jnp.concatenate([high, low, high], axis=0),
                preferred_element_type=jnp.float32,
            )
            loadings.append(split(factor))
    total = jnp.zeros((2 * (rows + rank), 2 * rank), jnp.float32)
    for group, (high, low) in enumerate(loadings):
        copies[group].wait()
        x_high, x_low = split(held_ref[group])
        total += lax.dot_general(
            jnp.concatenate([x_high, high, x_low, low], axis=0),
            jnp.concatenate([high, low], axis=0),
            (((1,), (1,)), ((), ())), preferred_element_type=jnp.float32,
        )
    total = total[:, :rank] + total[:, rank:]
    return total[: rows + rank] + total[rows + rank :]


def near_body(
    nyhi, nz, nx, place_ref, inverse_ref, x_ref, own_ref, left_ref, right_ref, total_ref,
    held_ref, sems,
):
    places = own_ref.shape[0]
    chunks = [
        (distance, [ref[i] for i in range(places)])
        for distance, ref in ((0, own_ref), (nx - 1, left_ref), (1, right_ref))
    ]
    total_ref[...] = contracted_blocks(
        nyhi, nz, place_ref, inverse_ref[...], x_ref, chunks, held_ref, sems
    )


def far_body(
    nyhi, nz, place_ref, inverse_ref, own_ref, x_ref, first_ref, second_ref, near_ref,
    out_ref, own_out_ref, held_ref, sems,
):
    inverse = inverse_ref[...]
    rank = inverse.shape[0]
    own_out_ref[...] = jnp.dot(
        inverse, own_ref[...], precision=FULL, preferred_element_type=jnp.float32
    )
    blocks = [ref[i] for ref in (first_ref, second_ref) for i in range(ref.shape[0])]
    total = near_ref[...] + contracted_blocks(
        nyhi, nz, place_ref, inverse, x_ref, [(2, blocks)], held_ref, sems
    )
    rows = total.shape[0] - rank
    half, quarter = rows // 2, rank // 2
    packed = jnp.concatenate(
        [
            jnp.concatenate([total[:half], total[half:rows]], axis=1),
            jnp.concatenate([total[rows : rows + quarter], total[rows + quarter :]], axis=1),
        ],
        axis=0,
    )
    for i in range(out_ref.shape[0]):
        out_ref[i] = packed


def right_divide(gram, right):
    size, block = gram.shape[0], 8
    work = jnp.concatenate([gram, right], axis=0)
    lane = lax.broadcasted_iota(jnp.int32, (1, size), 1)
    for p in range(0, size, block):
        rows = [work[i : i + 1, :] for i in range(block)]
        d = {
            (i, j): jnp.broadcast_to(rows[i][:, p + j : p + j + 1], (1, size))
            for i in range(block)
            for j in range(i, block)
        }
        here = (lane >= p) & (lane < p + block)
        y = [
            jnp.where(here, jnp.where(lane == p + i, -1.0, 0.0), rows[i])
            for i in range(block)
        ]
        inverse, low = [], {}
        for i in range(block):
            inverse.append(1.0 / d[i, i])
            for j in range(i + 1, block):
                low[j, i] = d[i, j] * inverse[i]
            for j in range(i + 1, block):
                for k in range(j, block):
                    d[j, k] -= low[j, i] * d[i, k]
                y[j] -= low[j, i] * y[i]
        factors = [None] * block
        for i in reversed(range(block)):
            factors[i] = y[i] * inverse[i]
            for j in range(i + 1, block):
                factors[i] -= low[j, i] * factors[j]
        rest = work[block:]
        work = jnp.where(here, 0.0, rest)
        for i in range(block):
            work -= rest[:, p + i : p + i + 1] * factors[i]
    return work


def diagonals(gram):
    size = gram.shape[0]
    mask = lax.broadcasted_iota(jnp.int32, (size, size), 0) == lax.broadcasted_iota(
        jnp.int32, (size, size), 1
    )
    kept = jnp.where(mask, gram, 0.0)
    return jnp.sum(kept, axis=0, keepdims=True), jnp.sum(kept, axis=1, keepdims=True)


def night_body(
    meters, got_ref, gram_c_ref, spans_t_ref, own_ref, send_ref, raw_ref, gram_ref, columns_ref
):
    rank = gram_c_ref.shape[0]
    intervals = spans_t_ref.shape[0]
    got = got_ref[0]
    for i in range(1, got_ref.shape[0]):
        got += got_ref[i]
    half = got.shape[0] - rank // 2
    contracted = jnp.concatenate([got[:half, :rank], got[:half, rank:]], axis=0)
    gram = jnp.concatenate([got[half:, :rank], got[half:, rank:]], axis=0)
    along, down = diagonals(gram)
    along = jnp.sqrt(along / meters + EPS)
    down = jnp.sqrt(down / meters + EPS)
    gram = gram / down / along
    contracted = (contracted / along).reshape(-1, intervals, rank)
    products = jnp.sum(contracted * spans_t_ref[...][None], axis=1)
    raw = right_divide(gram * gram_c_ref[...], products)
    interval = contracted[0] * raw[0:1]
    for j in range(1, raw.shape[0]):
        interval += contracted[j] * raw[j : j + 1]
    packed = jnp.concatenate(
        [
            jnp.concatenate([raw, raw], axis=1),
            jnp.concatenate([interval[: intervals // 2], interval[intervals // 2 :]], axis=1),
        ],
        axis=0,
    )
    for i in range(send_ref.shape[0]):
        send_ref[i] = packed
    raw_ref[...] = raw
    gram_ref[...] = gram
    columns_ref[...] = own_ref[...] / down


def span_body(night_total, got_ref, raw_ref, gram_ref, evenings_ref, spans_ref):
    rank = gram_ref.shape[0]
    nights = raw_ref.shape[0]
    everything = got_ref[:, :nights, :][:, :, :rank].reshape(-1, rank)
    gram = lax.dot_general(
        everything, everything, (((0,), (0,)), ((), ())), precision=FULL,
        preferred_element_type=jnp.float32,
    )
    interval = jnp.sum(got_ref[:, nights:, :], axis=0)
    along, down = diagonals(gram)
    along = jnp.sqrt(along / night_total + EPS)
    down = jnp.sqrt(down / night_total + EPS)
    gram = gram / down / along
    interval = jnp.concatenate([interval[:, :rank], interval[:, rank:]], axis=0) / along
    raw = right_divide(gram * gram_ref[...], interval)
    scale = jnp.sqrt(jnp.mean(raw * raw, axis=0, keepdims=True) + EPS)
    evenings_ref[...] = raw_ref[...] / along
    spans_ref[...] = raw / scale


def exchange(blocks, axis):
    return lax.all_to_all(blocks, axis, 0, 0, tiled=True)


def butterfly(total, axis):
    size = lax.axis_size(axis)
    step = 1
    while step < size:
        total += lax.ppermute(total, axis, [(i, i ^ step) for i in range(size)])
        step *= 2
    return total


def on_device(readings, evenings, spans):
    rank, nights = evenings.shape
    _, intervals, meters = readings.shape
    nx, nyhi, nz = (lax.axis_size(a) for a in NIGHT)
    night_devices = nx * nyhi * nz
    share = meters // night_devices
    copies = lax.axis_size(GRP)
    x2 = readings.reshape(nights * intervals, meters)
    gram_c = jnp.dot(spans, spans.T, precision=FULL)
    places = nyhi * nz
    groups = nx * nyhi
    anywhere = pl.BlockSpec(memory_space=pl.ANY)
    held = pltpu.VMEM((groups, nights * intervals, nz * share), jnp.float32)
    blocks = pl.pallas_call(
        functools.partial(partial_body, nyhi, nz),
        out_shape=f32(nx, places, rank, share),
        in_specs=[VMEM, VMEM, anywhere],
        out_specs=anywhere,
        scratch_shapes=[
            held,
            pltpu.VMEM((nx, places, rank, share), jnp.float32),
            pltpu.SemaphoreType.DMA((groups,)),
            pltpu.SemaphoreType.DMA((nx,)),
        ],
        compiler_params=STREAM,
    )(evenings.T, spans.T, x2)

    square = f32(rank, rank)
    gram_b = jnp.dot(evenings, evenings.T, precision=FULL)
    gram_b = butterfly(gram_b, "z")
    joined, gram_b = call(
        join_body, (f32(places, rank, share), square), exchange(blocks, "x"), gram_b
    )
    gram_b = butterfly(gram_b, "x")
    own, send, gram_b = call(
        own_body, (f32(rank, share), f32(places, rank, share), square),
        exchange(joined, ZY), gram_b,
    )
    chunk = exchange(send, ZY)
    gram_b = butterfly(gram_b, "yhi")
    inverse = call(inverse_body, square, gram_b, gram_c)

    up = [(i, (i + 1) % nx) for i in range(nx)]
    down = [(i, (i - 1) % nx) for i in range(nx)]
    left = lax.ppermute(chunk, "x", up)
    right = lax.ppermute(chunk, "x", down)
    part = f32(places // 2, rank, share)
    first, second, inverse = call(relay_body, (part, part, square), left, right, inverse)
    first = lax.ppermute(first, "x", up)
    second = lax.ppermute(second, "x", down)
    place = jnp.stack([lax.axis_index("x"), jnp.int32(nx)]).astype(jnp.int32)
    smem = pl.BlockSpec(memory_space=pltpu.SMEM)

    def parts(groups):
        return [
            pltpu.VMEM((groups, nights * intervals, nz * share), jnp.float32),
            pltpu.SemaphoreType.DMA((groups,)),
        ]

    near = pl.pallas_call(
        functools.partial(near_body, nyhi, nz, nx),
        out_shape=f32(nights * intervals + rank, rank),
        in_specs=[smem, VMEM, anywhere, VMEM, VMEM, VMEM],
        out_specs=VMEM,
        scratch_shapes=parts(3 * nyhi),
        compiler_params=CONTRACT,
    )(place, inverse, x2, chunk, left, right)
    packed, own_raw = pl.pallas_call(
        functools.partial(far_body, nyhi, nz),
        out_shape=(f32(copies, (nights * intervals + rank) // 2, 2 * rank), f32(rank, share)),
        in_specs=[smem, VMEM, VMEM, anywhere, VMEM, VMEM, VMEM],
        out_specs=(VMEM, VMEM),
        scratch_shapes=parts(nyhi),
        compiler_params=CONTRACT,
    )(place, inverse, own, x2, first, second, near)
    send, raw, gram_a, own_columns = call(
        functools.partial(night_body, meters * copies),
        (
            f32(night_devices, nights + intervals // 2, 2 * rank),
            f32(nights, rank), square, f32(rank, share),
        ),
        exchange(packed, GRP), gram_c, spans.T, own_raw,
    )
    evenings_out, spans_out = call(
        functools.partial(span_body, nights * night_devices),
        (f32(nights, rank), f32(intervals, rank)),
        exchange(send, NIGHT), raw, gram_a,
    )
    return own_columns, evenings_out.T, spans_out.T


def solution(mesh):
    fine = Mesh(
        np.asarray(mesh.devices).reshape(tuple(SPLIT.values())), tuple(SPLIT)
    )
    in_specs = (P(NIGHT, None, GRP), P(None, NIGHT), P())
    out_specs = (P(None, GRP + NIGHT), P(None, NIGHT), P())
    return jax.shard_map(
        on_device, mesh=fine, in_specs=in_specs, out_specs=out_specs, check_vma=False
    )
```

```python
import functools

import jax
import jax.numpy as jnp
import numpy as np
from jax import lax
from jax.experimental import pallas as pl
from jax.experimental.pallas import tpu as pltpu
from jax.sharding import Mesh, PartitionSpec as P

FULL = lax.Precision.HIGHEST
EPS = 1e-06
GRP = ("ylo", "core")
NIGHT = ("x", "yhi", "z")
ZY = ("z", "yhi")
SPLIT = {"ylo": 4, "core": 2, "x": 4, "yhi": 2, "z": 8}
VMEM = pl.BlockSpec(memory_space=pltpu.VMEM)
STREAM = pltpu.CompilerParams(vmem_limit_bytes=60 * 1024 * 1024)
CONTRACT = pltpu.CompilerParams(vmem_limit_bytes=50 * 1024 * 1024)
PARAMS = pltpu.CompilerParams(vmem_limit_bytes=40 * 1024 * 1024)


def f32(*shape):
    return jax.ShapeDtypeStruct(shape, jnp.float32)


def call(body, outs, *operands, params=PARAMS):
    return pl.pallas_call(
        body,
        out_shape=outs,
        in_specs=[VMEM] * len(operands),
        out_specs=jax.tree.map(lambda _: VMEM, outs),
        compiler_params=params,
    )(*operands)


def split(values):
    high = values.astype(jnp.bfloat16)
    return high, (values - high.astype(jnp.float32)).astype(jnp.bfloat16)


def transposed_dot(left, right):
    return lax.dot_general(
        left, right, (((0,), (0,)), ((), ())), precision=FULL,
        preferred_element_type=jnp.float32,
    )


def partial_body(
    nyhi, nz, nights_ref, spans_ref, x_ref, out_ref, held_ref, made_ref, in_sems, out_sems
):
    nights, rank = nights_ref.shape
    intervals = spans_ref.shape[0]
    share = out_ref.shape[-1]
    groups, width = held_ref.shape[0], nz * share
    arrivals = [
        pltpu.make_async_copy(
            x_ref.at[:, pl.ds(group * width, width)], held_ref.at[group], in_sems.at[group]
        )
        for group in range(groups)
    ]
    for copy in arrivals:
        copy.start()
    columns = nights * intervals
    kron = transposed_dot(
        nights_ref[...], onehot(nights, columns, lambda j, c: c // intervals == j)
    ) * transposed_dot(
        spans_ref[...], onehot(intervals, columns, lambda k, c: c % intervals == k)
    )
    high, low = split(kron)
    left = jnp.concatenate(
        [
            jnp.concatenate([high, high], axis=1),
            jnp.concatenate([low, jnp.zeros_like(low)], axis=1),
        ],
        axis=0,
    )
    departures = []
    for group in range(groups):
        x, y = group // nyhi, group % nyhi
        arrivals[group].wait()
        right = jnp.concatenate(split(held_ref[group]), axis=0)
        product = jnp.dot(left, right, preferred_element_type=jnp.float32)
        product = product[:rank] + product[rank:]
        for z in range(nz):
            made_ref[x, z * nyhi + y] = product[:, z * share : (z + 1) * share]
        if y == nyhi - 1:
            copy = pltpu.make_async_copy(made_ref.at[x], out_ref.at[x], out_sems.at[x])
            copy.start()
            departures.append(copy)
    for copy in departures:
        copy.wait()


def inverse_body(gram_b_ref, gram_c_ref, out_ref):
    gram = gram_b_ref[...] * gram_c_ref[...]
    out_ref[...] = right_divide(gram, identity(gram.shape[0]))


def join_body(got_ref, gram_ref, out_ref, gram_out_ref):
    for n in range(out_ref.shape[0]):
        block = got_ref[0, n]
        for i in range(1, got_ref.shape[0]):
            block += got_ref[i, n]
        out_ref[n] = block
    gram_out_ref[...] = gram_ref[...]


def own_body(got_ref, gram_ref, own_ref, send_ref, gram_out_ref):
    products = got_ref[0]
    for i in range(1, got_ref.shape[0]):
        products += got_ref[i]
    own_ref[...] = products
    for i in range(send_ref.shape[0]):
        send_ref[i] = products
    gram_out_ref[...] = gram_ref[...]


def relay_body(left_ref, right_ref, inverse_ref, first_ref, second_ref, inverse_out_ref):
    half = first_ref.shape[0]
    first_ref[...] = left_ref[:half]
    second_ref[...] = right_ref[half:]
    inverse_out_ref[...] = inverse_ref[...]


def onehot(rows, columns, test):
    return test(
        lax.broadcasted_iota(jnp.int32, (rows, columns), 0),
        lax.broadcasted_iota(jnp.int32, (rows, columns), 1),
    ).astype(jnp.float32)


def identity(size):
    return onehot(size, size, lambda i, j: i == j)


def contracted_blocks(nyhi, nz, place_ref, inverse, x_ref, chunks, held_ref, sems):
    nx = place_ref[1]
    rank, share = chunks[0][1][0].shape
    rows, width = held_ref.shape[1:]
    copies = []
    for distance, _ in chunks:
        x = lax.rem(place_ref[0] + distance, nx)
        for y in range(nyhi):
            start = pl.multiple_of((x * nyhi + y) * width, width)
            at = len(copies)
            copies.append(
                pltpu.make_async_copy(
                    x_ref.at[:, pl.ds(start, width)], held_ref.at[at], sems.at[at]
                )
            )
    for copy in copies:
        copy.start()
    high, low = split(inverse)
    solver = jnp.concatenate([high, high, low], axis=1)
    loadings = []
    for _, blocks in chunks:
        for y in range(nyhi):
            high, low = split(
                jnp.concatenate([blocks[z * nyhi + y] for z in range(nz)], axis=1)
            )
            factor = jnp.dot(
                solver, jnp.concatenate([high, low, high], axis=0),
                preferred_element_type=jnp.float32,
            )
            loadings.append(split(factor))
    total = jnp.zeros((2 * (rows + rank), 2 * rank), jnp.float32)
    for group, (high, low) in enumerate(loadings):
        copies[group].wait()
        x_high, x_low = split(held_ref[group])
        total += lax.dot_general(
            jnp.concatenate([x_high, high, x_low, low], axis=0),
            jnp.concatenate([high, low], axis=0),
            (((1,), (1,)), ((), ())), preferred_element_type=jnp.float32,
        )
    total = total[:, :rank] + total[:, rank:]
    return total[: rows + rank] + total[rows + rank :]


def near_body(
    nyhi, nz, nx, place_ref, inverse_ref, mine_ref, x_ref, own_ref, left_ref, right_ref,
    total_ref, own_out_ref, held_ref, sems,
):
    own_out_ref[...] = jnp.dot(
        inverse_ref[...], mine_ref[...], precision=FULL, preferred_element_type=jnp.float32
    )
    places = own_ref.shape[0]
    chunks = [
        (distance, [ref[i] for i in range(places)])
        for distance, ref in ((0, own_ref), (nx - 1, left_ref), (1, right_ref))
    ]
    total_ref[...] = contracted_blocks(
        nyhi, nz, place_ref, inverse_ref[...], x_ref, chunks, held_ref, sems
    )


def far_body(
    nyhi, nz, place_ref, inverse_ref, x_ref, first_ref, second_ref, near_ref, out_ref,
    held_ref, sems,
):
    inverse = inverse_ref[...]
    rank = inverse.shape[0]
    blocks = [ref[i] for ref in (first_ref, second_ref) for i in range(ref.shape[0])]
    total = near_ref[...] + contracted_blocks(
        nyhi, nz, place_ref, inverse, x_ref, [(2, blocks)], held_ref, sems
    )
    rows = total.shape[0] - rank
    half, quarter = rows // 2, rank // 2
    packed = jnp.concatenate(
        [
            jnp.concatenate([total[:half], total[half:rows]], axis=1),
            jnp.concatenate([total[rows : rows + quarter], total[rows + quarter :]], axis=1),
        ],
        axis=0,
    )
    for i in range(out_ref.shape[0]):
        out_ref[i] = packed


def right_divide(gram, right):
    size, block = gram.shape[0], 8
    work = jnp.concatenate([gram, right], axis=0)
    lane = lax.broadcasted_iota(jnp.int32, (1, size), 1)
    for p in range(0, size, block):
        rows = [work[i : i + 1, :] for i in range(block)]
        d = {
            (i, j): jnp.broadcast_to(rows[i][:, p + j : p + j + 1], (1, size))
            for i in range(block)
            for j in range(i, block)
        }
        here = (lane >= p) & (lane < p + block)
        y = [
            jnp.where(here, jnp.where(lane == p + i, -1.0, 0.0), rows[i])
            for i in range(block)
        ]
        inverse, low = [], {}
        for i in range(block):
            inverse.append(1.0 / d[i, i])
            for j in range(i + 1, block):
                low[j, i] = d[i, j] * inverse[i]
            for j in range(i + 1, block):
                for k in range(j, block):
                    d[j, k] -= low[j, i] * d[i, k]
                y[j] -= low[j, i] * y[i]
        factors = [None] * block
        for i in reversed(range(block)):
            factors[i] = y[i] * inverse[i]
            for j in range(i + 1, block):
                factors[i] -= low[j, i] * factors[j]
        rest = work[block:]
        work = jnp.where(here, 0.0, rest)
        for i in range(block):
            work -= rest[:, p + i : p + i + 1] * factors[i]
    return work


def diagonals(gram):
    size = gram.shape[0]
    mask = lax.broadcasted_iota(jnp.int32, (size, size), 0) == lax.broadcasted_iota(
        jnp.int32, (size, size), 1
    )
    kept = jnp.where(mask, gram, 0.0)
    return jnp.sum(kept, axis=0, keepdims=True), jnp.sum(kept, axis=1, keepdims=True)


def night_body(
    meters, got_ref, gram_c_ref, spans_t_ref, own_ref, send_ref, raw_ref, gram_ref, columns_ref
):
    rank = gram_c_ref.shape[0]
    intervals = spans_t_ref.shape[0]
    got = got_ref[0]
    for i in range(1, got_ref.shape[0]):
        got += got_ref[i]
    half = got.shape[0] - rank // 2
    contracted = jnp.concatenate([got[:half, :rank], got[:half, rank:]], axis=0)
    gram = jnp.concatenate([got[half:, :rank], got[half:, rank:]], axis=0)
    along, down = diagonals(gram)
    along = jnp.sqrt(along / meters + EPS)
    down = jnp.sqrt(down / meters + EPS)
    gram = gram / down / along
    contracted = (contracted / along).reshape(-1, intervals, rank)
    products = jnp.sum(contracted * spans_t_ref[...][None], axis=1)
    raw = right_divide(gram * gram_c_ref[...], products)
    interval = contracted[0] * raw[0:1]
    for j in range(1, raw.shape[0]):
        interval += contracted[j] * raw[j : j + 1]
    packed = jnp.concatenate(
        [
            jnp.concatenate([raw, raw], axis=1),
            jnp.concatenate([interval[: intervals // 2], interval[intervals // 2 :]], axis=1),
        ],
        axis=0,
    )
    for i in range(send_ref.shape[0]):
        send_ref[i] = packed
    raw_ref[...] = raw
    gram_ref[...] = gram
    columns_ref[...] = own_ref[...] / down


def span_body(night_total, got_ref, raw_ref, gram_ref, evenings_ref, spans_ref):
    rank = gram_ref.shape[0]
    nights = raw_ref.shape[0]
    everything = got_ref[:, :nights, :][:, :, :rank].reshape(-1, rank)
    gram = lax.dot_general(
        everything, everything, (((0,), (0,)), ((), ())), precision=FULL,
        preferred_element_type=jnp.float32,
    )
    interval = jnp.sum(got_ref[:, nights:, :], axis=0)
    along, down = diagonals(gram)
    along = jnp.sqrt(along / night_total + EPS)
    down = jnp.sqrt(down / night_total + EPS)
    gram = gram / down / along
    interval = jnp.concatenate([interval[:, :rank], interval[:, rank:]], axis=0) / along
    raw = right_divide(gram * gram_ref[...], interval)
    scale = jnp.sqrt(jnp.mean(raw * raw, axis=0, keepdims=True) + EPS)
    evenings_ref[...] = raw_ref[...] / along
    spans_ref[...] = raw / scale


def exchange(blocks, axis):
    return lax.all_to_all(blocks, axis, 0, 0, tiled=True)


def butterfly(total, axis):
    size = lax.axis_size(axis)
    step = 1
    while step < size:
        total += lax.ppermute(total, axis, [(i, i ^ step) for i in range(size)])
        step *= 2
    return total


def on_device(readings, evenings, spans):
    rank, nights = evenings.shape
    _, intervals, meters = readings.shape
    nx, nyhi, nz = (lax.axis_size(a) for a in NIGHT)
    night_devices = nx * nyhi * nz
    share = meters // night_devices
    copies = lax.axis_size(GRP)
    x2 = readings.reshape(nights * intervals, meters)
    gram_c = jnp.dot(spans, spans.T, precision=FULL)
    places = nyhi * nz
    groups = nx * nyhi
    anywhere = pl.BlockSpec(memory_space=pl.ANY)
    held = pltpu.VMEM((groups, nights * intervals, nz * share), jnp.float32)
    blocks = pl.pallas_call(
        functools.partial(partial_body, nyhi, nz),
        out_shape=f32(nx, places, rank, share),
        in_specs=[VMEM, VMEM, anywhere],
        out_specs=anywhere,
        scratch_shapes=[
            held,
            pltpu.VMEM((nx, places, rank, share), jnp.float32),
            pltpu.SemaphoreType.DMA((groups,)),
            pltpu.SemaphoreType.DMA((nx,)),
        ],
        compiler_params=STREAM,
    )(evenings.T, spans.T, x2)

    square = f32(rank, rank)
    gram_b = jnp.dot(evenings, evenings.T, precision=FULL)
    gram_b = butterfly(gram_b, "z")
    joined, gram_b = call(
        join_body, (f32(places, rank, share), square), exchange(blocks, "x"), gram_b
    )
    gram_b = butterfly(gram_b, "x")
    own, send, gram_b = call(
        own_body, (f32(rank, share), f32(places, rank, share), square),
        exchange(joined, ZY), gram_b,
    )
    chunk = exchange(send, ZY)
    gram_b = butterfly(gram_b, "yhi")
    inverse = call(inverse_body, square, gram_b, gram_c)

    up = [(i, (i + 1) % nx) for i in range(nx)]
    down = [(i, (i - 1) % nx) for i in range(nx)]
    left = lax.ppermute(chunk, "x", up)
    right = lax.ppermute(chunk, "x", down)
    part = f32(places // 2, rank, share)
    first, second, inverse = call(relay_body, (part, part, square), left, right, inverse)
    first = lax.ppermute(first, "x", up)
    second = lax.ppermute(second, "x", down)
    place = jnp.stack([lax.axis_index("x"), jnp.int32(nx)]).astype(jnp.int32)
    smem = pl.BlockSpec(memory_space=pltpu.SMEM)

    def parts(groups):
        return [
            pltpu.VMEM((groups, nights * intervals, nz * share), jnp.float32),
            pltpu.SemaphoreType.DMA((groups,)),
        ]

    near, own_raw = pl.pallas_call(
        functools.partial(near_body, nyhi, nz, nx),
        out_shape=(f32(nights * intervals + rank, rank), f32(rank, share)),
        in_specs=[smem, VMEM, VMEM, anywhere, VMEM, VMEM, VMEM],
        out_specs=(VMEM, VMEM),
        scratch_shapes=parts(3 * nyhi),
        compiler_params=CONTRACT,
    )(place, inverse, own, x2, chunk, left, right)
    packed = pl.pallas_call(
        functools.partial(far_body, nyhi, nz),
        out_shape=f32(copies, (nights * intervals + rank) // 2, 2 * rank),
        in_specs=[smem, VMEM, anywhere, VMEM, VMEM, VMEM],
        out_specs=VMEM,
        scratch_shapes=parts(nyhi),
        compiler_params=CONTRACT,
    )(place, inverse, x2, first, second, near)
    send, raw, gram_a, own_columns = call(
        functools.partial(night_body, meters * copies),
        (
            f32(night_devices, nights + intervals // 2, 2 * rank),
            f32(nights, rank), square, f32(rank, share),
        ),
        exchange(packed, GRP), gram_c, spans.T, own_raw,
    )
    evenings_out, spans_out = call(
        functools.partial(span_body, nights * night_devices),
        (f32(nights, rank), f32(intervals, rank)),
        exchange(send, NIGHT), raw, gram_a,
    )
    return own_columns, evenings_out.T, spans_out.T


def solution(mesh):
    fine = Mesh(
        np.asarray(mesh.devices).reshape(tuple(SPLIT.values())), tuple(SPLIT)
    )
    in_specs = (P(NIGHT, None, GRP), P(None, NIGHT), P())
    out_specs = (P(None, GRP + NIGHT), P(None, NIGHT), P())
    return jax.shard_map(
        on_device, mesh=fine, in_specs=in_specs, out_specs=out_specs, check_vma=False
    )
```
